32 devices in a mesh: expert: 4 (over z), hrow: 4 (over x, core), hcol: 2 (over y).
Axes of the slice: x: 2, y: 2, z: 4, core: 2. Of those that a mesh axis runs over, the one named last changes fastest.
Arguments:
- tokens: bfloat16 [256, 7168], P(('expert', 'hrow'), 'hcol')
- expert_ids: int32 [256, 8], P(('expert', 'hrow')), may hold values from 0 to 15, all different within a row; in each aligned block of 16 rows (0 to 15, 16 to 31, ...) at most 16 rows name the same one
- weight: bfloat16 [16, 256, 7168], P(('expert', 'hrow'), None, 'hcol'), may hold values from -6 to 6
- mask_bits: int32 [256, 224], P(None, 'hcol'), may hold values from -2147483648 to 2147483646, as said below
- damping: float32 [16, 7168], P(('expert', 'hrow'), 'hcol'), may hold values from 0.5 to 2
Outputs:
- new_weight: bfloat16 [16, 256, 7168], P(('expert', 'hrow'), None, 'hcol')
The draws below stay inside these ranges and needn't reach their ends.
Inputs may be any that keep to these rules, and one draw needn't show every extreme that they name: `expert_ids`: each token names 8 different experts; among the 16 rows of one device (aligned blocks of rows) no expert is named more than 16 times, a bound that some block reaches. `mask_bits`: every bit of every word is a keep flag (1 keeps the entry, 0 prunes it).
All inputs are finite; a program needn't handle non-finite values.
Results may differ from the reference program's by a relative error of at most 0.0044.
Values may be sent and summed in bfloat16 or wider, within the bound.
A program may use at most 64 MiB of HBM per device.

```python
import math
import jax
import jax.numpy as jnp
import numpy as np
from jax import lax

HD = 7168
TOPK = 8
SLAB = 256
EXP_DEV = 1
TOK_DEV = 16
EXPERTS = 16
TOKENS = 256
CAP = 16
ROWS_E = 128


def draw_tokens(key, part):
    key_base = jax.random.fold_in(key, 11)
    key_rows = jax.random.fold_in(key, 12)
    key_cols = jax.random.fold_in(key, 13)
    base = jax.random.truncated_normal(key_base, -4.0, 4.0, (TOKENS, HD), jnp.float32)
    row_scale = jnp.exp(jax.random.uniform(key_rows, (TOKENS, 1), jnp.float32, math.log(0.5), math.log(1.6)))
    col_scale = jnp.exp(jax.random.uniform(key_cols, (1, HD), jnp.float32, math.log(0.5), math.log(1.6)))
    return (base * row_scale * col_scale).astype(jnp.bfloat16)


def draw_mask_bits(key, part):
    return jax.random.randint(jax.random.fold_in(key, 21), (SLAB, HD // 32), -2147483648, 2147483647, jnp.int32)


def shard_levels(own_key, dims, split, smallest, largest):
    level = 1.0
    for position, parts in split:
        heights = jax.random.uniform(jax.random.fold_in(jax.random.fold_in(own_key, 6), position), (parts,), jnp.float32, smallest / len(split), largest / len(split))
        level = level * jnp.repeat(jnp.exp(heights), dims[position] // parts).reshape((-1,) + (1,) * (len(dims) - 1 - position))
    return level


def shared_out(rng, own, number, rows, count, top, reach, slope):
    ranking = jax.random.permutation(rng, count)
    packed, ordinary = shares(count, rows * top, reach, slope, True), shares(count, rows * top, reach, slope, False)
    places = jnp.arange(count)

    def named(lengths, offset_by):
        used = int((lengths > 0).sum())
        fixed = max(1, used // 4)
        passed = fixed + (places - fixed + offset_by * (used - fixed)) % max(1, count - fixed)
        return jnp.zeros((count,), jnp.int32).at[ranking[jnp.where(places < fixed, places, passed)]].set(jnp.asarray(lengths, jnp.int32))

    lengths = jnp.where(number % 4 == 0, named(packed, number // 4), named(ordinary, number - number // 4 - 1))
    mixed = jax.random.permutation(jax.random.fold_in(own, 3), count)
    giver, sink = mixed[0:count // 2 * 2:2], mixed[1:count // 2 * 2:2]
    room = jnp.minimum(lengths[giver] - 1, reach - lengths[sink]) // 2
    room = jnp.where((giver == ranking[0]) | (sink == ranking[0]) | (lengths[sink] == 0), 0, jnp.maximum(room, 0))
    passed = jax.random.randint(jax.random.fold_in(own, 4), (count // 2,), 0, 1 << 20) % (room + 1)
    lengths = lengths.at[giver].add(-passed).at[sink].add(passed)
    labels = jnp.searchsorted(jnp.cumsum(lengths), jnp.arange(rows * top), side="right").astype(jnp.int32)
    grid = labels.reshape(top, rows).T
    grid = grid[jax.random.permutation(jax.random.fold_in(own, 1), rows)]
    offset_by = jax.random.randint(jax.random.fold_in(own, 2), (rows, 1), 0, top)
    return jnp.take_along_axis(grid, (jnp.arange(top)[None, :] + offset_by) % top, axis=1)


def shares(number_of, total, reach, skew, full):
    weights = [(1 << 20) // math.isqrt(grade ** skew) + 1 for grade in range(1, number_of + 1)]
    largest = reach if full else min(reach, max(-(-total // number_of), total * weights[0] // sum(weights)))
    least = 1 if total - largest >= number_of - 1 else 0
    given, surplus = [largest] + [least] * (number_of - 1), total - largest - least * (number_of - 1)
    while surplus > 0:
        free = [i for i in range(1, number_of) if given[i] < largest] or [i for i in range(1, number_of) if given[i] < reach]
        pool, left = sum([weights[i] for i in free]), surplus
        for i in free:
            more = min(reach - given[i], max(1, left * weights[i] // pool), surplus)
            given[i] = given[i] + more
            surplus = surplus - more
    return np.array(given)


def gaussian(stream_key, extent, spread, limit, split=(), kind=jnp.bfloat16):
    result = spread * jax.random.normal(stream_key, extent, jnp.float32)
    if split:
        result = result * shard_levels(stream_key, extent, split, -0.22, 0.18)
    return jnp.clip(result, -limit, limit).astype(kind)


def setup_inputs(seed: int = 0) -> dict:
    arg_keys = jax.random.split(jax.random.key(seed), 6)
    tokens = draw_tokens(jax.random.fold_in(arg_keys[5], 71), 0)
    expert_ids_keys = jax.random.split(jax.random.fold_in(arg_keys[1], 1), TOKENS // TOK_DEV)
    expert_ids_turns = jax.random.permutation(jax.random.fold_in(arg_keys[1], 3), TOKENS // TOK_DEV)
    expert_ids = jax.vmap(lambda own, number: shared_out(jax.random.fold_in(arg_keys[1], 2), own, number, TOK_DEV, EXPERTS, TOPK, CAP, 2))(expert_ids_keys, expert_ids_turns).reshape((TOKENS, TOPK))
    weight = gaussian(arg_keys[2], (EXPERTS, SLAB, HD), 1.0, 6.0, ((0, 16), (2, 2)))
    mask_bits = draw_mask_bits(jax.random.fold_in(arg_keys[5], 71), 0)
    damping = jnp.clip(jnp.exp(math.log(2.0) - 1.3862944 * jax.random.uniform(arg_keys[4], (EXPERTS, HD), jnp.float32) ** shard_levels(arg_keys[4], (EXPERTS, HD), ((0, 16), (1, 2)), -0.2, 0.2)), 0.5, 2.0)
    return {"tokens": tokens, "expert_ids": expert_ids, "weight": weight, "mask_bits": mask_bits, "damping": damping}


ETA = 0.5


def unpack_bits(bits):
    bit_shifts = jnp.arange(32, dtype=jnp.int32)
    bit_flags = jnp.bitwise_and(jnp.right_shift(bits[:, :, None], bit_shifts[None, None, :]), 1)
    return bit_flags.reshape(bits.shape[0], bits.shape[1] * 32)


def reference(tokens, expert_ids, weight, mask_bits, damping):
    keep_flags = unpack_bits(mask_bits)
    max_rows = (EXPERTS // EXP_DEV) * CAP

    def one_expert(inputs):
        expert, slab, lam_row = inputs
        member = jnp.any(expert_ids == expert, axis=1)
        picked = jnp.nonzero(member, size=max_rows, fill_value=0)[0].astype(jnp.int32)
        live_count = jnp.sum(member.astype(jnp.int32))
        valid = (jnp.arange(max_rows, dtype=jnp.int32) < live_count).astype(jnp.float32)
        routed = tokens[picked].astype(jnp.float32) * valid[:, None]
        pruned = jnp.where(keep_flags == 1, jnp.float32(0.0), slab.astype(jnp.float32))
        projected = lax.dot_general(pruned, routed, (((1,), (1,)), ((), ())), precision=lax.Precision.HIGHEST)
        projected = lax.optimization_barrier(projected.astype(jnp.bfloat16)).astype(jnp.float32)
        comp_term = jnp.dot(projected, routed, precision=lax.Precision.HIGHEST) / ROWS_E
        diag_scale = jnp.sum(routed * routed, axis=0) / ROWS_E + lam_row
        updated = slab.astype(jnp.float32) + ETA * comp_term / diag_scale[None, :]
        return jnp.where(keep_flags == 1, updated, jnp.float32(0.0)).astype(jnp.bfloat16)

    return lax.map(one_expert, (jnp.arange(EXPERTS, dtype=jnp.int32), weight, damping))
```

```python
import functools

import jax
import jax.numpy as jnp
from jax import lax
from jax.experimental import pallas as pl
from jax.experimental.pallas import tpu as pltpu
from jax.sharding import PartitionSpec as P

ROWS_E = 128


ETA = 0.5


def unpack_bits(bits):
    bit_shifts = jnp.arange(32, dtype=jnp.int32)
    bit_flags = jnp.bitwise_and(jnp.right_shift(bits[:, :, None], bit_shifts[None, None, :]), 1)
    return bit_flags.reshape(bits.shape[0], bits.shape[1] * 32)


def route_rows(tokens, expert_ids, group_count, local_count):
    tok_count, top_count = expert_ids.shape
    expert_count = group_count * local_count
    capacity = 2 * tok_count * top_count // expert_count
    flat_ids = expert_ids.reshape(-1)
    one_hot = (flat_ids[:, None] == jnp.arange(expert_count, dtype=jnp.int32)[None, :]).astype(
        jnp.int32
    )
    prior_count = jnp.cumsum(one_hot, axis=0) - one_hot
    slot_index = jnp.sum(prior_count * one_hot, axis=1)
    group_of = flat_ids // local_count
    local_of = flat_ids % local_count
    target_slot = ((local_of * group_count + group_of) * capacity + slot_index).reshape(
        tok_count, top_count
    )
    slot_ids = jnp.arange(expert_count * capacity, dtype=jnp.int32)
    selector = jnp.any(slot_ids[:, None, None] == target_slot[None, :, :], axis=2).astype(
        jnp.bfloat16
    )
    packed = jnp.dot(selector, tokens, preferred_element_type=jnp.float32).astype(jnp.bfloat16)
    return packed.reshape(local_count, group_count, 1, capacity, tokens.shape[1])


def local(tokens, expert_ids, weight, mask_bits, damping):
    group_count = lax.axis_size(("expert", "hrow"))
    local_experts = weight.shape[0]
    feat_width = tokens.shape[1]
    slab_rows = weight.shape[1]
    packed = route_rows(tokens, expert_ids, group_count, local_experts)
    keep_flags = unpack_bits(mask_bits)
    keep_mask = keep_flags[None, :, :] == 1
    pruned = jnp.where(keep_mask, jnp.zeros_like(weight), weight)
    block = lax.all_to_all(packed, ("expert", "hrow"), split_axis=1, concat_axis=2, tiled=True)
    partials = jnp.einsum("esf,exgcf->exgcs", pruned, block, preferred_element_type=jnp.float32)
    slot_count = block.shape[1] * block.shape[2] * block.shape[3]
    routed = block.reshape(local_experts, slot_count, feat_width)
    partials = partials.reshape(local_experts, slot_count, slab_rows)
    projected = lax.psum(partials, "hcol").astype(jnp.bfloat16)
    comp_term = (
        jnp.einsum("ers,erf->esf", projected, routed, preferred_element_type=jnp.float32) / ROWS_E
    )
    diag_scale = (
        jnp.einsum("erf,erf->ef", routed, routed, preferred_element_type=jnp.float32) / ROWS_E
        + damping
    )
    updated = weight.astype(jnp.float32) + ETA * comp_term / diag_scale[:, None, :]
    return jnp.where(keep_mask, updated, jnp.float32(0.0)).astype(jnp.bfloat16)


MESH = pl.DeviceIdType.MESH
FLAGS = 128
CHUNK = 256


def kernel(tok_hbm, ids_hbm, w_hbm, bits_hbm, damp_hbm, out_hbm,
           held, w_ref, pruned, keep, part, other, squares, ids_ref, bits_ref, words, damp_ref, out_ref,
           load_sem, recv_sem, x_sem, core_sem, pair_sem, inner_sem, y_send, y_recv, store_sem):
    z, cross, y = lax.axis_index("expert"), lax.axis_index("hrow"), lax.axis_index("hcol")
    tok_count, feat = tok_hbm.shape
    slab = w_hbm.shape[1]
    half = feat // 256 * 128
    spans = ((0, half), (half, feat + FLAGS - half))
    x, core = cross // 2, cross % 2
    upper = z // 2
    inner = (z + 1) // 2 % 2
    mate = 4 * upper + 1 - z
    across = 3 - z
    order = (z, mate, 2 - upper, 3 - 3 * upper)
    x_row, core_row = (1 - x) * 2 + core, x * 2 + 1 - core
    both_row = (1 - x) * 2 + 1 - core
    to_mate, to_across = (mate, cross, y), (across, cross, y)
    to_x, to_core, to_y = (z, x_row, y), (z, core_row, y), (z, cross, 1 - y)
    mine = z * 4 + cross

    loads = [
        pltpu.make_async_copy(tok_hbm, held.at[mine, :, pl.ds(0, feat)], load_sem.at[0]),
        pltpu.make_async_copy(ids_hbm, ids_ref, load_sem.at[1]),
        pltpu.make_async_copy(bits_hbm, bits_ref, load_sem.at[2]),
        pltpu.make_async_copy(w_hbm.at[0], w_ref, load_sem.at[3]),
        pltpu.make_async_copy(damp_hbm, damp_ref, load_sem.at[4]),
    ]
    barrier = pltpu.get_barrier_semaphore()
    for device in (to_mate, to_x, to_core, to_y):
        pl.semaphore_signal(barrier, inc=1, device_id=device, device_id_type=MESH)

    @pl.when(inner == 1)
    def _():
        pl.semaphore_signal(barrier, inc=1, device_id=to_across, device_id_type=MESH)

    for load in loads:
        load.start()

    def block(number, h, sem, device):
        lo, size = spans[h]
        piece = held.at[number, :, pl.ds(lo, size)]
        return pltpu.make_async_remote_copy(
            src_ref=piece, dst_ref=piece, send_sem=sem, recv_sem=recv_sem.at[number, h],
            device_id=device, device_id_type=MESH)

    def arrived(number, h):
        block(number, h, x_sem.at[0, 0], to_x).wait_recv()

    always, inners = [], []

    def send(number, h, sem, device):
        copy = block(number, h, sem, device)
        copy.start()
        always.append(copy)

    def forward(step, number, h):
        if step == 0:
            send(number, h, pair_sem.at[0, h], to_mate)
        else:
            where, sem = ((to_across, inner_sem.at[1, h]) if step == 1 else (to_mate, pair_sem.at[step, h]))

            @pl.when(inner == 1)
            def _():
                block(number, h, sem, where).start()

            inners.append(block(number, h, sem, where))
        if step == 0:

            @pl.when(inner == 1)
            def _():
                block(number, h, inner_sem.at[0, h], to_across).start()

            inners.append(block(number, h, inner_sem.at[0, h], to_across))
        if not (step == 1 and h == 1):
            send(number, h, x_sem.at[step, h], to_x)
        send(number, h, core_sem.at[step, h], to_core)

    def crossed(step):
        number = order[step] * 4 + x_row
        for h in (0, 1):
            arrived(number, h)
            if step == 0 and h == 1:
                send(number, h, pair_sem.at[1, 0], to_mate)
            send(number, h, core_sem.at[4 + step, h], to_core)

    def column(step):
        number = order[step] * 4 + cross
        for h in (0, 1):
            arrived(number, h)
            forward(step, number, h)

    def plane_of(step):
        rows = 4 * tok_count
        return pl.ds(pl.multiple_of(order[step] * rows, rows), rows)

    def y_copy(step):
        rows = plane_of(step)
        return pltpu.make_async_remote_copy(
            src_ref=part.at[rows, :], dst_ref=other.at[rows, :], send_sem=y_send.at[step],
            recv_sem=y_recv.at[step], device_id=to_y, device_id_type=MESH)

    def member(flags):
        lane = lax.broadcasted_iota(jnp.int32, flags.shape, 1)
        return jnp.sum(jnp.where(lane == mine, flags.astype(jnp.float32), 0.0), axis=1, keepdims=True)

    def project(step):
        for h in (0, 1):
            arrived(order[step] * 4 + core_row, h)
            arrived(order[step] * 4 + both_row, h)
        rows = plane_of(step)
        blocks = pl.ds(order[step] * 4, 4)
        tokens = held[blocks, :, 0:feat].reshape(4 * tok_count, feat)
        part[rows, :] = lax.dot_general(
            tokens, pruned[...], (((1,), (1,)), ((), ())), preferred_element_type=jnp.float32)
        y_copy(step).start()
        here = member(held[blocks, :, feat:feat + FLAGS].reshape(4 * tok_count, FLAGS))
        for lo in range(0, feat, CHUNK):
            piece = held[blocks, :, lo:lo + CHUNK].reshape(4 * tok_count, CHUNK).astype(jnp.float32)
            total = jnp.sum((piece * piece * here).reshape(-1, 8, CHUNK), axis=0)
            squares[:, lo:lo + CHUNK] = total if step == 0 else squares[:, lo:lo + CHUNK] + total

    loads[1].wait()
    ids = ids_ref[...]
    lane = lax.broadcasted_iota(jnp.int32, (tok_count, FLAGS), 1)
    named = jnp.zeros((tok_count, FLAGS), jnp.float32)
    for k in range(ids.shape[1]):
        named = jnp.where(ids[:, k:k + 1] == lane, 1.0, named)
    held[mine, :, feat:feat + FLAGS] = named.astype(jnp.bfloat16)
    loads[0].wait()
    pl.semaphore_wait(barrier, 4 + inner)

    for h in (0, 1):
        forward(0, mine, h)

    loads[2].wait()
    loads[3].wait()
    words[...] = jnp.zeros_like(words)
    words[:, 0:bits_ref.shape[1]] = bits_ref[...]

    def unpack(j, carry):
        at = pl.ds(pl.multiple_of(j * 128, 128), 128)
        spot = lax.broadcasted_iota(jnp.int32, (slab, 128), 1)
        word = jnp.take_along_axis(words[...], 4 * j + spot // 32, axis=1)
        bit = jnp.bitwise_and(jnp.right_shift(word, spot % 32), 1)
        flag = bit.astype(jnp.float32)
        keep[:, at] = flag.astype(jnp.bfloat16)
        pruned[:, at] = jnp.where(bit == 1, 0.0, w_ref[:, at].astype(jnp.float32)).astype(jnp.bfloat16)
        return carry

    lax.fori_loop(0, feat // 128, unpack, 0)
    loads[4].wait()

    column(1)
    crossed(0)
    project(0)
    column(2)
    crossed(1)
    project(1)
    column(3)
    crossed(2)
    project(2)
    crossed(3)
    project(3)

    here = member(held[:, :, feat:feat + FLAGS].reshape(-1, FLAGS))
    for step in range(4):
        y_copy(step).wait_recv()
    projected = jnp.where(here > 0.5, part[...] + other[...], 0.0).T.astype(jnp.bfloat16)
    stores = []
    for lo in range(0, feat, CHUNK):
        at = slice(lo, lo + CHUNK)
        routed = held[:, :, at].reshape(-1, CHUNK)
        comp = jnp.dot(projected, routed, preferred_element_type=jnp.float32)
        diag = jnp.sum(squares[:, at], axis=0, keepdims=True) / ROWS_E + damp_ref[:, at]
        updated = w_ref[:, at].astype(jnp.float32) + comp * (ETA / ROWS_E / diag)
        out_ref[:, at] = updated.astype(jnp.bfloat16) * keep[:, at]
        store = pltpu.make_async_copy(out_ref.at[:, at], out_hbm.at[0, :, at], store_sem.at[lo // CHUNK])
        store.start()
        stores.append(store)

    for copy in always:
        copy.wait_send()
    for step in range(4):
        y_copy(step).wait_send()

    @pl.when(inner == 1)
    def _():
        for copy in inners:
            copy.wait_send()

    for store in stores:
        store.wait()


def gathered(tokens, expert_ids, weight, mask_bits, damping):
    tok_count, feat = tokens.shape
    slab = weight.shape[1]
    blocks = 16
    total = blocks * tok_count
    dma = pltpu.SemaphoreType.DMA
    return pl.pallas_call(
        kernel,
        out_shape=jax.ShapeDtypeStruct(weight.shape, jnp.bfloat16),
        in_specs=[pl.BlockSpec(memory_space=pl.ANY)] * 5,
        out_specs=pl.BlockSpec(memory_space=pl.ANY),
        scratch_shapes=[
            pltpu.VMEM((blocks, tok_count, feat + FLAGS), jnp.bfloat16),
            pltpu.VMEM((slab, feat), jnp.bfloat16),
            pltpu.VMEM((slab, feat), jnp.bfloat16),
            pltpu.VMEM((slab, feat), jnp.bfloat16),
            pltpu.VMEM((total, slab), jnp.float32),
            pltpu.VMEM((total, slab), jnp.float32),
            pltpu.VMEM((8, feat), jnp.float32),
            pltpu.VMEM(expert_ids.shape, jnp.int32),
            pltpu.VMEM(mask_bits.shape, jnp.int32),
            pltpu.VMEM((slab, 128), jnp.int32),
            pltpu.VMEM((1, feat), jnp.float32),
            pltpu.VMEM((slab, feat), jnp.bfloat16),
            dma((5,)),
            dma((blocks, 2)),
            dma((4, 2)),
            dma((8, 2)),
            dma((4, 2)),
            dma((2, 2)),
            dma((4,)),
            dma((4,)),
            dma((feat // CHUNK,)),
        ],
        compiler_params=pltpu.CompilerParams(
            collective_id=0, has_side_effects=True, vmem_limit_bytes=40 * 1024 * 1024),
        cost_estimate=pl.CostEstimate(
            flops=4 * total * slab * feat, bytes_accessed=4 * slab * feat, transcendentals=0),
    )(tokens, expert_ids, weight, mask_bits, damping)


def solution(mesh):
    in_specs = (
        P(("expert", "hrow"), "hcol"),
        P(("expert", "hrow"), None),
        P(("expert", "hrow"), None, "hcol"),
        P(None, "hcol"),
        P(("expert", "hrow"), "hcol"),
    )
    out_specs = P(("expert", "hrow"), None, "hcol")
    line, cross = mesh.shape["expert"], mesh.shape["hrow"]

    def body(tokens, expert_ids, weight, mask_bits, damping):
        tok_count, top_count = expert_ids.shape
        capacity = 2 * tok_count * top_count // (line * cross * weight.shape[0])
        fits = line == 4 and cross == 4 and mesh.shape["hcol"] == 2 and weight.shape[0] == 1
        if fits and capacity >= tok_count:
            return gathered(tokens, expert_ids, weight, mask_bits, damping)
        return local(tokens, expert_ids, weight, mask_bits, damping)

    return jax.shard_map(body, mesh=mesh, in_specs=in_specs, out_specs=out_specs, check_vma=False)
```

```python
import functools

import jax
import jax.numpy as jnp
from jax import lax
from jax.experimental import pallas as pl
from jax.experimental.pallas import tpu as pltpu
from jax.sharding import PartitionSpec as P

ROWS_E = 128


ETA = 0.5


def unpack_bits(bits):
    bit_shifts = jnp.arange(32, dtype=jnp.int32)
    bit_flags = jnp.bitwise_and(jnp.right_shift(bits[:, :, None], bit_shifts[None, None, :]), 1)
    return bit_flags.reshape(bits.shape[0], bits.shape[1] * 32)


def route_rows(tokens, expert_ids, group_count, local_count):
    tok_count, top_count = expert_ids.shape
    expert_count = group_count * local_count
    capacity = 2 * tok_count * top_count // expert_count
    flat_ids = expert_ids.reshape(-1)
    one_hot = (flat_ids[:, None] == jnp.arange(expert_count, dtype=jnp.int32)[None, :]).astype(
        jnp.int32
    )
    prior_count = jnp.cumsum(one_hot, axis=0) - one_hot
    slot_index = jnp.sum(prior_count * one_hot, axis=1)
    group_of = flat_ids // local_count
    local_of = flat_ids % local_count
    target_slot = ((local_of * group_count + group_of) * capacity + slot_index).reshape(
        tok_count, top_count
    )
    slot_ids = jnp.arange(expert_count * capacity, dtype=jnp.int32)
    selector = jnp.any(slot_ids[:, None, None] == target_slot[None, :, :], axis=2).astype(
        jnp.bfloat16
    )
    packed = jnp.dot(selector, tokens, preferred_element_type=jnp.float32).astype(jnp.bfloat16)
    return packed.reshape(local_count, group_count, 1, capacity, tokens.shape[1])


def local(tokens, expert_ids, weight, mask_bits, damping):
    group_count = lax.axis_size(("expert", "hrow"))
    local_experts = weight.shape[0]
    feat_width = tokens.shape[1]
    slab_rows = weight.shape[1]
    packed = route_rows(tokens, expert_ids, group_count, local_experts)
    keep_flags = unpack_bits(mask_bits)
    keep_mask = keep_flags[None, :, :] == 1
    pruned = jnp.where(keep_mask, jnp.zeros_like(weight), weight)
    block = lax.all_to_all(packed, ("expert", "hrow"), split_axis=1, concat_axis=2, tiled=True)
    partials = jnp.einsum("esf,exgcf->exgcs", pruned, block, preferred_element_type=jnp.float32)
    slot_count = block.shape[1] * block.shape[2] * block.shape[3]
    routed = block.reshape(local_experts, slot_count, feat_width)
    partials = partials.reshape(local_experts, slot_count, slab_rows)
    projected = lax.psum(partials, "hcol").astype(jnp.bfloat16)
    comp_term = (
        jnp.einsum("ers,erf->esf", projected, routed, preferred_element_type=jnp.float32) / ROWS_E
    )
    diag_scale = (
        jnp.einsum("erf,erf->ef", routed, routed, preferred_element_type=jnp.float32) / ROWS_E
        + damping
    )
    updated = weight.astype(jnp.float32) + ETA * comp_term / diag_scale[:, None, :]
    return jnp.where(keep_mask, updated, jnp.float32(0.0)).astype(jnp.bfloat16)


MESH = pl.DeviceIdType.MESH
FLAGS = 128
CHUNK = 256


def kernel(tok_hbm, ids_hbm, w_hbm, bits_hbm, damp_hbm, out_hbm,
           held, w_ref, pruned, keep, part, other, squares, ids_ref, wide_ids, bits_ref, words, damp_ref, out_ref,
           load_sem, recv_sem, x_sem, core_sem, mate_sem, far_sem, across_sem, y_send, y_recv, store_sem):
    z, cross, y = lax.axis_index("expert"), lax.axis_index("hrow"), lax.axis_index("hcol")
    tok_count, feat = tok_hbm.shape
    slab = w_hbm.shape[1]
    half = feat // 256 * 128
    spans = ((0, half), (half, feat + FLAGS - half))
    x, core = cross // 2, cross % 2
    upper = z // 2
    inner = (z + 1) // 2 % 2
    mate = 4 * upper + 1 - z
    across = 3 - z
    far = (z + 2) % 4
    order = (z, mate, 2 - upper, 3 - 3 * upper)
    x_row, core_row = (1 - x) * 2 + core, x * 2 + 1 - core
    both_row = (1 - x) * 2 + 1 - core
    to_mate, to_across, to_far = (mate, cross, y), (across, cross, y), (far, cross, y)
    to_first = (mate * inner + far * (1 - inner), cross, y)
    to_second = (far * inner + mate * (1 - inner), cross, y)
    to_x, to_core, to_y = (z, x_row, y), (z, core_row, y), (z, cross, 1 - y)
    mine = z * 4 + cross

    loads = [
        pltpu.make_async_copy(tok_hbm, held.at[mine, :, pl.ds(0, feat)], load_sem.at[0]),
        pltpu.make_async_copy(ids_hbm, ids_ref, load_sem.at[1]),
        pltpu.make_async_copy(bits_hbm, bits_ref.at[pl.ds(0, bits_hbm.shape[0]), :], load_sem.at[2]),
        pltpu.make_async_copy(w_hbm.at[0], w_ref, load_sem.at[3]),
        pltpu.make_async_copy(damp_hbm, damp_ref, load_sem.at[4]),
    ]
    barrier = pltpu.get_barrier_semaphore()
    for device in (to_mate, to_far, to_x, to_core, to_y):
        pl.semaphore_signal(barrier, inc=1, device_id=device, device_id_type=MESH)

    @pl.when(inner == 1)
    def _():
        pl.semaphore_signal(barrier, inc=1, device_id=to_across, device_id_type=MESH)

    for load in loads:
        load.start()

    def block(number, h, sem, device):
        lo, size = spans[h]
        piece = held.at[number, :, pl.ds(lo, size)]
        return pltpu.make_async_remote_copy(
            src_ref=piece, dst_ref=piece, send_sem=sem, recv_sem=recv_sem.at[number, h],
            device_id=device, device_id_type=MESH)

    def arrived(number, h):
        block(number, h, x_sem.at[0, 0], to_x).wait_recv()

    always, inners = [], []

    def send(number, h, sem, device):
        copy = block(number, h, sem, device)
        copy.start()
        always.append(copy)

    def spread(number, h):
        send(number, h, x_sem.at[0, h], to_x)

        @pl.when(inner == 1)
        def _():
            block(number, h, across_sem.at[h], to_across).start()

        inners.append(block(number, h, across_sem.at[h], to_across))
        send(number, h, mate_sem.at[0, h], to_first)
        send(number, h, far_sem.at[h], to_second)
        send(number, h, core_sem.at[0, h], to_core)

    def column(step):
        number = order[step] * 4 + cross
        for h in (0, 1):
            arrived(number, h)
            if step == 3:

                @pl.when(inner == 1)
                def _():
                    block(number, h, mate_sem.at[2, h], to_mate).start()

                inners.append(block(number, h, mate_sem.at[2, h], to_mate))
            if not (step == 1 and h == 1):
                send(number, h, x_sem.at[step, h], to_x)
            send(number, h, core_sem.at[step, h], to_core)

    def crossed(step):
        number = order[step] * 4 + x_row
        for h in (0, 1):
            arrived(number, h)
            if step == 0 and h == 1:
                send(number, h, mate_sem.at[1, 0], to_mate)
            send(number, h, core_sem.at[4 + step, h], to_core)

    def rows_of(first, count):
        return pl.ds(pl.multiple_of(first * tok_count, tok_count), count * tok_count)

    def y_copy(first, count, which):
        rows = rows_of(first, count)
        return pltpu.make_async_remote_copy(
            src_ref=part.at[rows, :], dst_ref=other.at[rows, :], send_sem=y_send.at[which],
            recv_sem=y_recv.at[which], device_id=to_y, device_id_type=MESH)

    def member(flags):
        lane = lax.broadcasted_iota(jnp.int32, flags.shape, 1)
        return jnp.sum(jnp.where(lane == mine, flags.astype(jnp.float32), 0.0), axis=1, keepdims=True)

    summed = []

    def project(first, count):
        rows, blocks = count * tok_count, pl.ds(first, count)
        tokens = held[blocks, :, 0:feat].reshape(rows, feat)
        part[rows_of(first, count), :] = lax.dot_general(
            tokens, pruned[...], (((1,), (1,)), ((), ())), preferred_element_type=jnp.float32)
        copy = y_copy(first, count, len(summed))
        copy.start()
        summed.append(copy)
        here = member(held[blocks, :, feat:feat + FLAGS].reshape(rows, FLAGS))
        for lo in range(0, feat, CHUNK):
            piece = held[blocks, :, lo:lo + CHUNK].reshape(rows, CHUNK).astype(jnp.float32)
            total = jnp.sum((piece * piece * here).reshape(-1, 8, CHUNK), axis=0)
            squares[:, lo:lo + CHUNK] = total if len(summed) == 1 else squares[:, lo:lo + CHUNK] + total

    def other_core(step, row):
        for h in (0, 1):
            arrived(order[step] * 4 + row, h)

    def plane(step):
        other_core(step, core_row)
        other_core(step, both_row)
        project(order[step] * 4, 4)

    loads[1].wait()
    wide_ids[...] = jnp.full_like(wide_ids, -1)
    wide_ids[:, 0:tok_count] = ids_ref[...]
    expert = lax.broadcasted_iota(jnp.int32, (FLAGS, 128), 0)
    named = jnp.zeros((FLAGS, 128), jnp.float32)
    for k in range(ids_ref.shape[0]):
        named = jnp.where(wide_ids[k:k + 1, :] == expert, 1.0, named)
    held[mine, :, feat:feat + FLAGS] = named.T[0:tok_count, :].astype(jnp.bfloat16)
    loads[0].wait()
    pl.semaphore_wait(barrier, 5 + inner)

    for h in (0, 1):
        spread(mine, h)

    filled = bits_hbm.shape[0]
    if filled < 128:
        bits_ref[filled:128, :] = jnp.zeros((128 - filled, slab), jnp.int32)
    loads[2].wait()
    loads[3].wait()
    words[...] = bits_ref[...].T

    def unpack(j, carry):
        at = pl.ds(pl.multiple_of(j * 128, 128), 128)
        spot = lax.broadcasted_iota(jnp.int32, (slab, 128), 1)
        word = jnp.take_along_axis(words[...], 4 * j + spot // 32, axis=1)
        bit = jnp.bitwise_and(jnp.right_shift(word, spot % 32), 1)
        flag = bit.astype(jnp.float32)
        keep[:, at] = flag.astype(jnp.bfloat16)
        pruned[:, at] = jnp.where(bit == 1, 0.0, w_ref[:, at].astype(jnp.float32)).astype(jnp.bfloat16)
        return carry

    steps = feat // 128
    lax.fori_loop(0, steps // 2, unpack, 0)
    column(1)
    crossed(0)
    lax.fori_loop(steps // 2, steps, unpack, 0)
    column(2)
    crossed(1)
    plane(0)
    plane(1)
    column(3)
    crossed(2)
    plane(2)
    other_core(3, core_row)
    project(order[3] * 4 + 2 * x, 2)
    crossed(3)
    other_core(3, both_row)
    project(order[3] * 4 + 2 * (1 - x), 2)

    loads[4].wait()
    here = member(held[:, :, feat:feat + FLAGS].reshape(-1, FLAGS))
    for copy in summed:
        copy.wait_recv()
    projected = jnp.where(here > 0.5, part[...] + other[...], 0.0).T.astype(jnp.bfloat16)
    stores = []
    for lo in range(0, feat, CHUNK):
        at = slice(lo, lo + CHUNK)
        routed = held[:, :, at].reshape(-1, CHUNK)
        comp = jnp.dot(projected, routed, preferred_element_type=jnp.float32)
        diag = jnp.sum(squares[:, at], axis=0, keepdims=True) / ROWS_E + damp_ref[:, at]
        updated = w_ref[:, at].astype(jnp.float32) + comp * (ETA / ROWS_E / diag)
        out_ref[:, at] = updated.astype(jnp.bfloat16) * keep[:, at]
        store = pltpu.make_async_copy(out_ref.at[:, at], out_hbm.at[0, :, at], store_sem.at[lo // CHUNK])
        store.start()
        stores.append(store)

    for copy in always:
        copy.wait_send()
    for copy in summed:
        copy.wait_send()

    @pl.when(inner == 1)
    def _():
        for copy in inners:
            copy.wait_send()

    for store in stores:
        store.wait()


def gathered(tokens, expert_ids, weight, mask_bits, damping):
    tok_count, feat = tokens.shape
    slab = weight.shape[1]
    blocks = 16
    total = blocks * tok_count
    dma = pltpu.SemaphoreType.DMA
    return pl.pallas_call(
        kernel,
        out_shape=jax.ShapeDtypeStruct(weight.shape, jnp.bfloat16),
        in_specs=[pl.BlockSpec(memory_space=pltpu.HBM)] * 5,
        out_specs=pl.BlockSpec(memory_space=pl.ANY),
        scratch_shapes=[
            pltpu.VMEM((blocks, tok_count, feat + FLAGS), jnp.bfloat16),
            pltpu.VMEM((slab, feat), jnp.bfloat16),
            pltpu.VMEM((slab, feat), jnp.bfloat16),
            pltpu.VMEM((slab, feat), jnp.bfloat16),
            pltpu.VMEM((total, slab), jnp.float32),
            pltpu.VMEM((total, slab), jnp.float32),
            pltpu.VMEM((8, feat), jnp.float32),
            pltpu.VMEM((expert_ids.shape[1], tok_count), jnp.int32),
            pltpu.VMEM((expert_ids.shape[1], 128), jnp.int32),
            pltpu.VMEM((128, slab), jnp.int32),
            pltpu.VMEM((slab, 128), jnp.int32),
            pltpu.VMEM((1, feat), jnp.float32),
            pltpu.VMEM((slab, feat), jnp.bfloat16),
            dma((5,)),
            dma((blocks, 2)),
            dma((4, 2)),
            dma((8, 2)),
            dma((3, 2)),
            dma((2,)),
            dma((2,)),
            dma((5,)),
            dma((5,)),
            dma((feat // CHUNK,)),
        ],
        compiler_params=pltpu.CompilerParams(
            collective_id=0, has_side_effects=True, vmem_limit_bytes=63 * 1024 * 1024),
        cost_estimate=pl.CostEstimate(
            flops=4 * total * slab * feat, bytes_accessed=4 * slab * feat, transcendentals=0),
    )(tokens, expert_ids.T, weight, mask_bits.T, damping)


def solution(mesh):
    in_specs = (
        P(("expert", "hrow"), "hcol"),
        P(("expert", "hrow"), None),
        P(("expert", "hrow"), None, "hcol"),
        P(None, "hcol"),
        P(("expert", "hrow"), "hcol"),
    )
    out_specs = P(("expert", "hrow"), None, "hcol")
    line, cross = mesh.shape["expert"], mesh.shape["hrow"]

    def body(tokens, expert_ids, weight, mask_bits, damping):
        tok_count, top_count = expert_ids.shape
        capacity = 2 * tok_count * top_count // (line * cross * weight.shape[0])
        fits = line == 4 and cross == 4 and mesh.shape["hcol"] == 2 and weight.shape[0] == 1
        if fits and capacity >= tok_count:
            return gathered(tokens, expert_ids, weight, mask_bits, damping)
        return local(tokens, expert_ids, weight, mask_bits, damping)

    return jax.shard_map(body, mesh=mesh, in_specs=in_specs, out_specs=out_specs, check_vma=False)
```

```python
import functools

import jax
import jax.numpy as jnp
from jax import lax
from jax.experimental import pallas as pl
from jax.experimental.pallas import tpu as pltpu
from jax.sharding import PartitionSpec as P

ROWS_E = 128


ETA = 0.5


def unpack_bits(bits):
    bit_shifts = jnp.arange(32, dtype=jnp.int32)
    bit_flags = jnp.bitwise_and(jnp.right_shift(bits[:, :, None], bit_shifts[None, None, :]), 1)
    return bit_flags.reshape(bits.shape[0], bits.shape[1] * 32)


def route_rows(tokens, expert_ids, group_count, local_count):
    tok_count, top_count = expert_ids.shape
    expert_count = group_count * local_count
    capacity = 2 * tok_count * top_count // expert_count
    flat_ids = expert_ids.reshape(-1)
    one_hot = (flat_ids[:, None] == jnp.arange(expert_count, dtype=jnp.int32)[None, :]).astype(
        jnp.int32
    )
    prior_count = jnp.cumsum(one_hot, axis=0) - one_hot
    slot_index = jnp.sum(prior_count * one_hot, axis=1)
    group_of = flat_ids // local_count
    local_of = flat_ids % local_count
    target_slot = ((local_of * group_count + group_of) * capacity + slot_index).reshape(
        tok_count, top_count
    )
    slot_ids = jnp.arange(expert_count * capacity, dtype=jnp.int32)
    selector = jnp.any(slot_ids[:, None, None] == target_slot[None, :, :], axis=2).astype(
        jnp.bfloat16
    )
    packed = jnp.dot(selector, tokens, preferred_element_type=jnp.float32).astype(jnp.bfloat16)
    return packed.reshape(local_count, group_count, 1, capacity, tokens.shape[1])


def local(tokens, expert_ids, weight, mask_bits, damping):
    group_count = lax.axis_size(("expert", "hrow"))
    local_experts = weight.shape[0]
    feat_width = tokens.shape[1]
    slab_rows = weight.shape[1]
    packed = route_rows(tokens, expert_ids, group_count, local_experts)
    keep_flags = unpack_bits(mask_bits)
    keep_mask = keep_flags[None, :, :] == 1
    pruned = jnp.where(keep_mask, jnp.zeros_like(weight), weight)
    block = lax.all_to_all(packed, ("expert", "hrow"), split_axis=1, concat_axis=2, tiled=True)
    partials = jnp.einsum("esf,exgcf->exgcs", pruned, block, preferred_element_type=jnp.float32)
    slot_count = block.shape[1] * block.shape[2] * block.shape[3]
    routed = block.reshape(local_experts, slot_count, feat_width)
    partials = partials.reshape(local_experts, slot_count, slab_rows)
    projected = lax.psum(partials, "hcol").astype(jnp.bfloat16)
    comp_term = (
        jnp.einsum("ers,erf->esf", projected, routed, preferred_element_type=jnp.float32) / ROWS_E
    )
    diag_scale = (
        jnp.einsum("erf,erf->ef", routed, routed, preferred_element_type=jnp.float32) / ROWS_E
        + damping
    )
    updated = weight.astype(jnp.float32) + ETA * comp_term / diag_scale[:, None, :]
    return jnp.where(keep_mask, updated, jnp.float32(0.0)).astype(jnp.bfloat16)


MESH = pl.DeviceIdType.MESH
FLAGS = 128
CHUNK = 256
WIDE = 512


def kernel(tok_hbm, ids_hbm, w_hbm, bits_hbm, damp_hbm, out_hbm,
           held, w_ref, pruned, keep, part, other, squares, ids_ref, wide_ids, bits_ref, words, damp_ref, out_ref,
           load_sem, recv_sem, x_sem, core_sem, mate_sem, far_sem, across_sem, y_send, y_recv, store_sem):
    z, cross, y = lax.axis_index("expert"), lax.axis_index("hrow"), lax.axis_index("hcol")
    tok_count, feat = tok_hbm.shape
    slab = w_hbm.shape[1]
    half = feat // 256 * 128
    spans = ((0, half), (half, feat + FLAGS - half))
    x, core = cross // 2, cross % 2
    upper = z // 2
    inner = (z + 1) // 2 % 2
    mate = 4 * upper + 1 - z
    across = 3 - z
    far = (z + 2) % 4
    order = (z, mate, 2 - upper, 3 - 3 * upper)
    x_row, core_row = (1 - x) * 2 + core, x * 2 + 1 - core
    both_row = (1 - x) * 2 + 1 - core
    to_mate, to_across, to_far = (mate, cross, y), (across, cross, y), (far, cross, y)
    to_first = (mate * inner + far * (1 - inner), cross, y)
    to_second = (far * inner + mate * (1 - inner), cross, y)
    to_x, to_core, to_y = (z, x_row, y), (z, core_row, y), (z, cross, 1 - y)
    mine = z * 4 + cross

    loads = [
        pltpu.make_async_copy(tok_hbm, held.at[mine, :, pl.ds(0, feat)], load_sem.at[0]),
        pltpu.make_async_copy(ids_hbm, ids_ref, load_sem.at[1]),
        pltpu.make_async_copy(bits_hbm, bits_ref.at[pl.ds(0, bits_hbm.shape[0]), :], load_sem.at[2]),
        pltpu.make_async_copy(w_hbm.at[0], w_ref, load_sem.at[3]),
        pltpu.make_async_copy(damp_hbm, damp_ref, load_sem.at[4]),
    ]
    barrier = pltpu.get_barrier_semaphore()
    for device in (to_mate, to_far, to_x, to_core, to_y):
        pl.semaphore_signal(barrier, inc=1, device_id=device, device_id_type=MESH)

    @pl.when(inner == 1)
    def _():
        pl.semaphore_signal(barrier, inc=1, device_id=to_across, device_id_type=MESH)

    for load in loads:
        load.start()

    def block(number, h, sem, device):
        lo, size = spans[h]
        piece = held.at[number, :, pl.ds(lo, size)]
        return pltpu.make_async_remote_copy(
            src_ref=piece, dst_ref=piece, send_sem=sem, recv_sem=recv_sem.at[number, h],
            device_id=device, device_id_type=MESH)

    def arrived(number, h):
        block(number, h, x_sem.at[0, 0], to_x).wait_recv()

    always, inners = [], []

    def send(number, h, sem, device):
        copy = block(number, h, sem, device)
        copy.start()
        always.append(copy)

    def spread(number, h):
        send(number, h, x_sem.at[0, h], to_x)

        @pl.when(inner == 1)
        def _():
            block(number, h, across_sem.at[h], to_across).start()

        inners.append(block(number, h, across_sem.at[h], to_across))
        send(number, h, mate_sem.at[0, h], to_first)
        send(number, h, far_sem.at[h], to_second)
        send(number, h, core_sem.at[0, h], to_core)

    def column(step):
        number = order[step] * 4 + cross
        for h in (0, 1):
            arrived(number, h)
            if step == 3:

                @pl.when(inner == 1)
                def _():
                    block(number, h, mate_sem.at[2, h], to_mate).start()

                inners.append(block(number, h, mate_sem.at[2, h], to_mate))
            if not (step == 1 and h == 1):
                send(number, h, x_sem.at[step, h], to_x)
            send(number, h, core_sem.at[step, h], to_core)

    def crossed(step):
        number = order[step] * 4 + x_row
        for h in (0, 1):
            arrived(number, h)
            if step == 0 and h == 1:
                send(number, h, mate_sem.at[1, 0], to_mate)
            send(number, h, core_sem.at[4 + step, h], to_core)

    def rows_of(first, count):
        return pl.ds(pl.multiple_of(first * tok_count, tok_count), count * tok_count)

    def y_copy(first, count, which):
        rows = rows_of(first, count)
        return pltpu.make_async_remote_copy(
            src_ref=part.at[rows, :], dst_ref=other.at[rows, :], send_sem=y_send.at[which],
            recv_sem=y_recv.at[which], device_id=to_y, device_id_type=MESH)

    def member(flags):
        lane = lax.broadcasted_iota(jnp.int32, flags.shape, 1)
        return jnp.sum(jnp.where(lane == mine, flags.astype(jnp.float32), 0.0), axis=1, keepdims=True)

    summed = []

    def project(first, count):
        rows, blocks = count * tok_count, pl.ds(first, count)
        tokens = held[blocks, :, 0:feat].reshape(rows, feat)
        part[rows_of(first, count), :] = lax.dot_general(
            pruned[...], tokens, (((1,), (1,)), ((), ())), preferred_element_type=jnp.float32).T
        copy = y_copy(first, count, len(summed))
        copy.start()
        summed.append(copy)
        here = member(held[blocks, :, feat:feat + FLAGS].reshape(rows, FLAGS))
        for lo in range(0, feat, CHUNK):
            piece = held[blocks, :, lo:lo + CHUNK].reshape(rows, CHUNK).astype(jnp.float32)
            total = jnp.sum((piece * piece * here).reshape(-1, 8, CHUNK), axis=0)
            squares[:, lo:lo + CHUNK] = total if len(summed) == 1 else squares[:, lo:lo + CHUNK] + total

    def other_core(step, row):
        for h in (0, 1):
            arrived(order[step] * 4 + row, h)

    def plane(step):
        other_core(step, core_row)
        other_core(step, both_row)
        project(order[step] * 4, 4)

    loads[1].wait()
    wide_ids[...] = jnp.full_like(wide_ids, -1)
    wide_ids[:, 0:tok_count] = ids_ref[...]
    expert = lax.broadcasted_iota(jnp.int32, (FLAGS, 128), 0)
    named = jnp.zeros((FLAGS, 128), jnp.float32)
    for k in range(ids_ref.shape[0]):
        named = jnp.where(wide_ids[k:k + 1, :] == expert, 1.0, named)
    held[mine, :, feat:feat + FLAGS] = named.T[0:tok_count, :].astype(jnp.bfloat16)
    loads[0].wait()
    pl.semaphore_wait(barrier, 5 + inner)

    for h in (0, 1):
        spread(mine, h)

    filled = bits_hbm.shape[0]
    if filled < 128:
        bits_ref[filled:128, :] = jnp.zeros((128 - filled, slab), jnp.int32)
    loads[2].wait()
    loads[3].wait()
    words[...] = bits_ref[...].T

    spot = lax.broadcasted_iota(jnp.int32, (1, 128), 1)
    group = jnp.right_shift(spot, 5)
    probe = jnp.left_shift(jnp.int32(1), jnp.bitwise_and(spot, 31))

    def unpack(j, carry):
        at = pl.ds(pl.multiple_of(j * 128, 128), 128)
        index = jnp.broadcast_to(group + 4 * j, (slab, 128))
        word = jnp.take_along_axis(words[...], index, axis=1)
        flag = jnp.where(jnp.bitwise_and(word, probe) != 0, 1.0, 0.0).astype(jnp.bfloat16)
        keep[:, at] = flag
        pruned[:, at] = w_ref[:, at] * (jnp.bfloat16(1.0) - flag)
        return carry

    steps = feat // 128
    lax.fori_loop(0, steps // 2, unpack, 0)
    column(1)
    crossed(0)
    lax.fori_loop(steps // 2, steps, unpack, 0)
    column(2)
    crossed(1)
    plane(0)
    plane(1)
    column(3)
    crossed(2)
    plane(2)
    other_core(3, core_row)
    project(order[3] * 4 + 2 * x, 2)
    crossed(3)
    other_core(3, both_row)
    project(order[3] * 4 + 2 * (1 - x), 2)

    loads[4].wait()
    here = member(held[:, :, feat:feat + FLAGS].reshape(-1, FLAGS))
    for copy in summed:
        copy.wait_recv()
    projected = jnp.where(here > 0.5, part[...] + other[...], 0.0).T.astype(jnp.bfloat16)
    stores = []
    for lo in range(0, feat, WIDE):
        at = slice(lo, lo + WIDE)
        routed = held[:, :, at].reshape(-1, WIDE)
        comp = jnp.dot(projected, routed, preferred_element_type=jnp.float32)
        diag = jnp.sum(squares[:, at], axis=0, keepdims=True) / ROWS_E + damp_ref[:, at]
        updated = w_ref[:, at].astype(jnp.float32) + comp * (ETA / ROWS_E / diag)
        out_ref[:, at] = updated.astype(jnp.bfloat16) * keep[:, at]
        store = pltpu.make_async_copy(out_ref.at[:, at], out_hbm.at[0, :, at], store_sem.at[lo // WIDE])
        store.start()
        stores.append(store)

    for copy in always:
        copy.wait_send()
    for copy in summed:
        copy.wait_send()

    @pl.when(inner == 1)
    def _():
        for copy in inners:
            copy.wait_send()

    for store in stores:
        store.wait()


def gathered(tokens, expert_ids, weight, mask_bits, damping):
    tok_count, feat = tokens.shape
    slab = weight.shape[1]
    blocks = 16
    total = blocks * tok_count
    dma = pltpu.SemaphoreType.DMA
    return pl.pallas_call(
        kernel,
        out_shape=jax.ShapeDtypeStruct(weight.shape, jnp.bfloat16),
        in_specs=[pl.BlockSpec(memory_space=pltpu.HBM)] * 5,
        out_specs=pl.BlockSpec(memory_space=pl.ANY),
        scratch_shapes=[
            pltpu.VMEM((blocks, tok_count, feat + FLAGS), jnp.bfloat16),
            pltpu.VMEM((slab, feat), jnp.bfloat16),
            pltpu.VMEM((slab, feat), jnp.bfloat16),
            pltpu.VMEM((slab, feat), jnp.bfloat16),
            pltpu.VMEM((total, slab), jnp.float32),
            pltpu.VMEM((total, slab), jnp.float32),
            pltpu.VMEM((8, feat), jnp.float32),
            pltpu.VMEM((expert_ids.shape[1], tok_count), jnp.int32),
            pltpu.VMEM((expert_ids.shape[1], 128), jnp.int32),
            pltpu.VMEM((128, slab), jnp.int32),
            pltpu.VMEM((slab, 128), jnp.int32),
            pltpu.VMEM((1, feat), jnp.float32),
            pltpu.VMEM((slab, feat), jnp.bfloat16),
            dma((5,)),
            dma((blocks, 2)),
            dma((4, 2)),
            dma((8, 2)),
            dma((3, 2)),
            dma((2,)),
            dma((2,)),
            dma((5,)),
            dma((5,)),
            dma((feat // WIDE,)),
        ],
        compiler_params=pltpu.CompilerParams(
            collective_id=0, has_side_effects=True, vmem_limit_bytes=62 * 1024 * 1024),
        cost_estimate=pl.CostEstimate(
            flops=4 * total * slab * feat, bytes_accessed=4 * slab * feat, transcendentals=0),
    )(tokens, expert_ids.T, weight, mask_bits.T, damping)


def solution(mesh):
    in_specs = (
        P(("expert", "hrow"), "hcol"),
        P(("expert", "hrow"), None),
        P(("expert", "hrow"), None, "hcol"),
        P(None, "hcol"),
        P(("expert", "hrow"), "hcol"),
    )
    out_specs = P(("expert", "hrow"), None, "hcol")
    line, cross = mesh.shape["expert"], mesh.shape["hrow"]

    def body(tokens, expert_ids, weight, mask_bits, damping):
        tok_count, top_count = expert_ids.shape
        capacity = 2 * tok_count * top_count // (line * cross * weight.shape[0])
        fits = line == 4 and cross == 4 and mesh.shape["hcol"] == 2 and weight.shape[0] == 1
        if fits and capacity >= tok_count:
            return gathered(tokens, expert_ids, weight, mask_bits, damping)
        return local(tokens, expert_ids, weight, mask_bits, damping)

    return jax.shard_map(body, mesh=mesh, in_specs=in_specs, out_specs=out_specs, check_vma=False)
```

```python
import functools

import jax
import jax.numpy as jnp
from jax import lax
from jax.experimental import pallas as pl
from jax.experimental.pallas import tpu as pltpu
from jax.sharding import PartitionSpec as P

ROWS_E = 128


ETA = 0.5


def unpack_bits(bits):
    bit_shifts = jnp.arange(32, dtype=jnp.int32)
    bit_flags = jnp.bitwise_and(jnp.right_shift(bits[:, :, None], bit_shifts[None, None, :]), 1)
    return bit_flags.reshape(bits.shape[0], bits.shape[1] * 32)


def route_rows(tokens, expert_ids, group_count, local_count):
    tok_count, top_count = expert_ids.shape
    expert_count = group_count * local_count
    capacity = 2 * tok_count * top_count // expert_count
    flat_ids = expert_ids.reshape(-1)
    one_hot = (flat_ids[:, None] == jnp.arange(expert_count, dtype=jnp.int32)[None, :]).astype(
        jnp.int32
    )
    prior_count = jnp.cumsum(one_hot, axis=0) - one_hot
    slot_index = jnp.sum(prior_count * one_hot, axis=1)
    group_of = flat_ids // local_count
    local_of = flat_ids % local_count
    target_slot = ((local_of * group_count + group_of) * capacity + slot_index).reshape(
        tok_count, top_count
    )
    slot_ids = jnp.arange(expert_count * capacity, dtype=jnp.int32)
    selector = jnp.any(slot_ids[:, None, None] == target_slot[None, :, :], axis=2).astype(
        jnp.bfloat16
    )
    packed = jnp.dot(selector, tokens, preferred_element_type=jnp.float32).astype(jnp.bfloat16)
    return packed.reshape(local_count, group_count, 1, capacity, tokens.shape[1])


def local(tokens, expert_ids, weight, mask_bits, damping):
    group_count = lax.axis_size(("expert", "hrow"))
    local_experts = weight.shape[0]
    feat_width = tokens.shape[1]
    slab_rows = weight.shape[1]
    packed = route_rows(tokens, expert_ids, group_count, local_experts)
    keep_flags = unpack_bits(mask_bits)
    keep_mask = keep_flags[None, :, :] == 1
    pruned = jnp.where(keep_mask, jnp.zeros_like(weight), weight)
    block = lax.all_to_all(packed, ("expert", "hrow"), split_axis=1, concat_axis=2, tiled=True)
    partials = jnp.einsum("esf,exgcf->exgcs", pruned, block, preferred_element_type=jnp.float32)
    slot_count = block.shape[1] * block.shape[2] * block.shape[3]
    routed = block.reshape(local_experts, slot_count, feat_width)
    partials = partials.reshape(local_experts, slot_count, slab_rows)
    projected = lax.psum(partials, "hcol").astype(jnp.bfloat16)
    comp_term = (
        jnp.einsum("ers,erf->esf", projected, routed, preferred_element_type=jnp.float32) / ROWS_E
    )
    diag_scale = (
        jnp.einsum("erf,erf->ef", routed, routed, preferred_element_type=jnp.float32) / ROWS_E
        + damping
    )
    updated = weight.astype(jnp.float32) + ETA * comp_term / diag_scale[:, None, :]
    return jnp.where(keep_mask, updated, jnp.float32(0.0)).astype(jnp.bfloat16)


MESH = pl.DeviceIdType.MESH
FLAGS = 128
CHUNK = 256
WIDE = 512


def kernel(tok_hbm, ids_hbm, w_hbm, bits_hbm, damp_hbm, out_hbm,
           held, w_ref, pruned, keep, part, other, squares, ids_ref, wide_ids, bits_ref, words, damp_ref, out_ref,
           load_sem, recv_sem, x_sem, core_sem, line_sem, y_send, y_recv, store_sem):
    z, cross, y = lax.axis_index("expert"), lax.axis_index("hrow"), lax.axis_index("hcol")
    tok_count, feat = tok_hbm.shape
    slab = w_hbm.shape[1]
    half = feat // 256 * 128
    spans = ((0, half), (half, feat + FLAGS - half))
    x, core = cross // 2, cross % 2
    upper = z // 2
    mate = 4 * upper + 1 - z
    order = (z, mate, 2 - upper, 3 - 3 * upper)
    x_row, core_row = (1 - x) * 2 + core, x * 2 + 1 - core
    both_row = (1 - x) * 2 + 1 - core
    to_mate = (mate, cross, y)
    to_line = [(order[step], cross, y) for step in (3, 2, 1)]
    to_x, to_core, to_y = (z, x_row, y), (z, core_row, y), (z, cross, 1 - y)
    mine = z * 4 + cross

    loads = [
        pltpu.make_async_copy(tok_hbm, held.at[mine, :, pl.ds(0, feat)], load_sem.at[0]),
        pltpu.make_async_copy(ids_hbm, ids_ref, load_sem.at[1]),
        pltpu.make_async_copy(bits_hbm, bits_ref.at[pl.ds(0, bits_hbm.shape[0]), :], load_sem.at[2]),
        pltpu.make_async_copy(w_hbm.at[0], w_ref, load_sem.at[3]),
        pltpu.make_async_copy(damp_hbm, damp_ref, load_sem.at[4]),
    ]
    barrier = pltpu.get_barrier_semaphore()
    for device in to_line + [to_x, to_core, to_y]:
        pl.semaphore_signal(barrier, inc=1, device_id=device, device_id_type=MESH)

    for load in loads:
        load.start()

    def block(number, h, sem, device):
        lo, size = spans[h]
        piece = held.at[number, :, pl.ds(lo, size)]
        return pltpu.make_async_remote_copy(
            src_ref=piece, dst_ref=piece, send_sem=sem, recv_sem=recv_sem.at[number, h],
            device_id=device, device_id_type=MESH)

    def arrived(number, h):
        block(number, h, x_sem.at[0, 0], to_x).wait_recv()

    always = []

    def send(number, h, sem, device):
        copy = block(number, h, sem, device)
        copy.start()
        always.append(copy)

    def spread(number, h):
        send(number, h, x_sem.at[0, h], to_x)
        for place, device in enumerate(to_line):
            send(number, h, line_sem.at[place, h], device)
        send(number, h, core_sem.at[0, h], to_core)

    def column(step):
        number = order[step] * 4 + cross
        for h in (0, 1):
            arrived(number, h)
            if not (step == 1 and h == 1):
                send(number, h, x_sem.at[step, h], to_x)
            send(number, h, core_sem.at[step, h], to_core)

    def crossed(step):
        number = order[step] * 4 + x_row
        for h in (0, 1):
            arrived(number, h)
            if step == 0 and h == 1:
                send(number, h, line_sem.at[3, 0], to_mate)
            send(number, h, core_sem.at[4 + step, h], to_core)

    def rows_of(first, count):
        return pl.ds(pl.multiple_of(first * tok_count, tok_count), count * tok_count)

    def y_copy(first, count, which):
        rows = rows_of(first, count)
        return pltpu.make_async_remote_copy(
            src_ref=part.at[rows, :], dst_ref=other.at[rows, :], send_sem=y_send.at[which],
            recv_sem=y_recv.at[which], device_id=to_y, device_id_type=MESH)

    def member(flags):
        lane = lax.broadcasted_iota(jnp.int32, flags.shape, 1)
        return jnp.sum(jnp.where(lane == mine, flags.astype(jnp.float32), 0.0), axis=1, keepdims=True)

    summed = []

    def project(first, count):
        rows, blocks = count * tok_count, pl.ds(first, count)
        tokens = held[blocks, :, 0:feat].reshape(rows, feat)
        part[rows_of(first, count), :] = lax.dot_general(
            pruned[...], tokens, (((1,), (1,)), ((), ())), preferred_element_type=jnp.float32).T
        copy = y_copy(first, count, len(summed))
        copy.start()
        summed.append(copy)
        here = member(held[blocks, :, feat:feat + FLAGS].reshape(rows, FLAGS))
        for lo in range(0, feat, CHUNK):
            piece = held[blocks, :, lo:lo + CHUNK].reshape(rows, CHUNK).astype(jnp.float32)
            total = jnp.sum((piece * piece * here).reshape(-1, 8, CHUNK), axis=0)
            squares[:, lo:lo + CHUNK] = total if len(summed) == 1 else squares[:, lo:lo + CHUNK] + total

    def other_core(step, row):
        for h in (0, 1):
            arrived(order[step] * 4 + row, h)

    def plane(step):
        other_core(step, core_row)
        other_core(step, both_row)
        project(order[step] * 4, 4)

    loads[1].wait()
    wide_ids[...] = jnp.full_like(wide_ids, -1)
    wide_ids[:, 0:tok_count] = ids_ref[...]
    expert = lax.broadcasted_iota(jnp.int32, (FLAGS, 128), 0)
    named = jnp.zeros((FLAGS, 128), jnp.float32)
    for k in range(ids_ref.shape[0]):
        named = jnp.where(wide_ids[k:k + 1, :] == expert, 1.0, named)
    held[mine, :, feat:feat + FLAGS] = named.T[0:tok_count, :].astype(jnp.bfloat16)
    loads[0].wait()
    pl.semaphore_wait(barrier, 6)

    for h in (0, 1):
        spread(mine, h)

    filled = bits_hbm.shape[0]
    if filled < 128:
        bits_ref[filled:128, :] = jnp.zeros((128 - filled, slab), jnp.int32)
    loads[2].wait()
    loads[3].wait()
    words[...] = bits_ref[...].T

    spot = lax.broadcasted_iota(jnp.int32, (1, 128), 1)
    group = jnp.right_shift(spot, 5)
    probe = jnp.left_shift(jnp.int32(1), jnp.bitwise_and(spot, 31))

    def unpack(j, carry):
        at = pl.ds(pl.multiple_of(j * 128, 128), 128)
        index = jnp.broadcast_to(group + 4 * j, (slab, 128))
        word = jnp.take_along_axis(words[...], index, axis=1)
        flag = jnp.where(jnp.bitwise_and(word, probe) != 0, 1.0, 0.0).astype(jnp.bfloat16)
        keep[:, at] = flag
        pruned[:, at] = w_ref[:, at] * (jnp.bfloat16(1.0) - flag)
        return carry

    steps = feat // 128
    lax.fori_loop(0, steps // 2, unpack, 0)
    column(1)
    crossed(0)
    lax.fori_loop(steps // 2, steps, unpack, 0)
    column(2)
    crossed(1)
    plane(0)
    plane(1)
    column(3)
    crossed(2)
    plane(2)
    other_core(3, core_row)
    project(order[3] * 4 + 2 * x, 2)
    crossed(3)
    other_core(3, both_row)
    project(order[3] * 4 + 2 * (1 - x), 2)

    loads[4].wait()
    here = member(held[:, :, feat:feat + FLAGS].reshape(-1, FLAGS))
    for copy in summed:
        copy.wait_recv()
    projected = jnp.where(here > 0.5, part[...] + other[...], 0.0).T.astype(jnp.bfloat16)
    stores = []
    for lo in range(0, feat, WIDE):
        at = slice(lo, lo + WIDE)
        routed = held[:, :, at].reshape(-1, WIDE)
        comp = jnp.dot(projected, routed, preferred_element_type=jnp.float32)
        diag = jnp.sum(squares[:, at], axis=0, keepdims=True) / ROWS_E + damp_ref[:, at]
        updated = w_ref[:, at].astype(jnp.float32) + comp * (ETA / ROWS_E / diag)
        out_ref[:, at] = updated.astype(jnp.bfloat16) * keep[:, at]
        store = pltpu.make_async_copy(out_ref.at[:, at], out_hbm.at[0, :, at], store_sem.at[lo // WIDE])
        store.start()
        stores.append(store)

    for copy in always:
        copy.wait_send()
    for copy in summed:
        copy.wait_send()

    for store in stores:
        store.wait()


def gathered(tokens, expert_ids, weight, mask_bits, damping):
    tok_count, feat = tokens.shape
    slab = weight.shape[1]
    blocks = 16
    total = blocks * tok_count
    dma = pltpu.SemaphoreType.DMA
    return pl.pallas_call(
        kernel,
        out_shape=jax.ShapeDtypeStruct(weight.shape, jnp.bfloat16),
        in_specs=[pl.BlockSpec(memory_space=pltpu.HBM)] * 5,
        out_specs=pl.BlockSpec(memory_space=pl.ANY),
        scratch_shapes=[
            pltpu.VMEM((blocks, tok_count, feat + FLAGS), jnp.bfloat16),
            pltpu.VMEM((slab, feat), jnp.bfloat16),
            pltpu.VMEM((slab, feat), jnp.bfloat16),
            pltpu.VMEM((slab, feat), jnp.bfloat16),
            pltpu.VMEM((total, slab), jnp.float32),
            pltpu.VMEM((total, slab), jnp.float32),
            pltpu.VMEM((8, feat), jnp.float32),
            pltpu.VMEM((expert_ids.shape[1], tok_count), jnp.int32),
            pltpu.VMEM((expert_ids.shape[1], 128), jnp.int32),
            pltpu.VMEM((128, slab), jnp.int32),
            pltpu.VMEM((slab, 128), jnp.int32),
            pltpu.VMEM((1, feat), jnp.float32),
            pltpu.VMEM((slab, feat), jnp.bfloat16),
            dma((5,)),
            dma((blocks, 2)),
            dma((4, 2)),
            dma((8, 2)),
            dma((4, 2)),
            dma((5,)),
            dma((5,)),
            dma((feat // WIDE,)),
        ],
        compiler_params=pltpu.CompilerParams(
            collective_id=0, has_side_effects=True, vmem_limit_bytes=62 * 1024 * 1024),
        cost_estimate=pl.CostEstimate(
            flops=4 * total * slab * feat, bytes_accessed=4 * slab * feat, transcendentals=0),
    )(tokens, expert_ids.T, weight, mask_bits.T, damping)


def solution(mesh):
    in_specs = (
        P(("expert", "hrow"), "hcol"),
        P(("expert", "hrow"), None),
        P(("expert", "hrow"), None, "hcol"),
        P(None, "hcol"),
        P(("expert", "hrow"), "hcol"),
    )
    out_specs = P(("expert", "hrow"), None, "hcol")
    line, cross = mesh.shape["expert"], mesh.shape["hrow"]

    def body(tokens, expert_ids, weight, mask_bits, damping):
        tok_count, top_count = expert_ids.shape
        capacity = 2 * tok_count * top_count // (line * cross * weight.shape[0])
        fits = line == 4 and cross == 4 and mesh.shape["hcol"] == 2 and weight.shape[0] == 1
        if fits and capacity >= tok_count:
            return gathered(tokens, expert_ids, weight, mask_bits, damping)
        return local(tokens, expert_ids, weight, mask_bits, damping)

    return jax.shard_map(body, mesh=mesh, in_specs=in_specs, out_specs=out_specs, check_vma=False)
```

```python
import functools

import jax
import jax.numpy as jnp
from jax import lax
from jax.experimental import pallas as pl
from jax.experimental.pallas import tpu as pltpu
from jax.sharding import PartitionSpec as P

ROWS_E = 128


ETA = 0.5


def unpack_bits(bits):
    bit_shifts = jnp.arange(32, dtype=jnp.int32)
    bit_flags = jnp.bitwise_and(jnp.right_shift(bits[:, :, None], bit_shifts[None, None, :]), 1)
    return bit_flags.reshape(bits.shape[0], bits.shape[1] * 32)


def route_rows(tokens, expert_ids, group_count, local_count):
    tok_count, top_count = expert_ids.shape
    expert_count = group_count * local_count
    capacity = 2 * tok_count * top_count // expert_count
    flat_ids = expert_ids.reshape(-1)
    one_hot = (flat_ids[:, None] == jnp.arange(expert_count, dtype=jnp.int32)[None, :]).astype(
        jnp.int32
    )
    prior_count = jnp.cumsum(one_hot, axis=0) - one_hot
    slot_index = jnp.sum(prior_count * one_hot, axis=1)
    group_of = flat_ids // local_count
    local_of = flat_ids % local_count
    target_slot = ((local_of * group_count + group_of) * capacity + slot_index).reshape(
        tok_count, top_count
    )
    slot_ids = jnp.arange(expert_count * capacity, dtype=jnp.int32)
    selector = jnp.any(slot_ids[:, None, None] == target_slot[None, :, :], axis=2).astype(
        jnp.bfloat16
    )
    packed = jnp.dot(selector, tokens, preferred_element_type=jnp.float32).astype(jnp.bfloat16)
    return packed.reshape(local_count, group_count, 1, capacity, tokens.shape[1])


def local(tokens, expert_ids, weight, mask_bits, damping):
    group_count = lax.axis_size(("expert", "hrow"))
    local_experts = weight.shape[0]
    feat_width = tokens.shape[1]
    slab_rows = weight.shape[1]
    packed = route_rows(tokens, expert_ids, group_count, local_experts)
    keep_flags = unpack_bits(mask_bits)
    keep_mask = keep_flags[None, :, :] == 1
    pruned = jnp.where(keep_mask, jnp.zeros_like(weight), weight)
    block = lax.all_to_all(packed, ("expert", "hrow"), split_axis=1, concat_axis=2, tiled=True)
    partials = jnp.einsum("esf,exgcf->exgcs", pruned, block, preferred_element_type=jnp.float32)
    slot_count = block.shape[1] * block.shape[2] * block.shape[3]
    routed = block.reshape(local_experts, slot_count, feat_width)
    partials = partials.reshape(local_experts, slot_count, slab_rows)
    projected = lax.psum(partials, "hcol").astype(jnp.bfloat16)
    comp_term = (
        jnp.einsum("ers,erf->esf", projected, routed, preferred_element_type=jnp.float32) / ROWS_E
    )
    diag_scale = (
        jnp.einsum("erf,erf->ef", routed, routed, preferred_element_type=jnp.float32) / ROWS_E
        + damping
    )
    updated = weight.astype(jnp.float32) + ETA * comp_term / diag_scale[:, None, :]
    return jnp.where(keep_mask, updated, jnp.float32(0.0)).astype(jnp.bfloat16)


MESH = pl.DeviceIdType.MESH
FLAGS = 128
CHUNK = 256
WIDE = 512


def kernel(tok_hbm, ids_hbm, w_hbm, bits_hbm, damp_hbm, out_hbm,
           held, w_ref, pruned, keep, part, other, squares, ids_ref, wide_ids, bits_ref, words, damp_ref, out_ref,
           load_sem, recv_sem, x_sem, core_sem, mate_sem, across_sem, y_send, y_recv, store_sem):
    z, cross, y = lax.axis_index("expert"), lax.axis_index("hrow"), lax.axis_index("hcol")
    tok_count, feat = tok_hbm.shape
    slab = w_hbm.shape[1]
    half = feat // 256 * 128
    spans = ((0, half), (half, feat + FLAGS - half))
    x, core = cross // 2, cross % 2
    upper = z // 2
    inner = (z + 1) // 2 % 2
    mate = 4 * upper + 1 - z
    across = 3 - z
    order = (z, mate, 2 - upper, 3 - 3 * upper)
    x_row, core_row = (1 - x) * 2 + core, x * 2 + 1 - core
    both_row = (1 - x) * 2 + 1 - core
    to_mate, to_across = (mate, cross, y), (across, cross, y)
    to_x, to_core, to_y = (z, x_row, y), (z, core_row, y), (z, cross, 1 - y)
    mine = z * 4 + cross

    loads = [
        pltpu.make_async_copy(tok_hbm, held.at[mine, :, pl.ds(0, feat)], load_sem.at[0]),
        pltpu.make_async_copy(ids_hbm, ids_ref, load_sem.at[1]),
        pltpu.make_async_copy(bits_hbm, bits_ref.at[pl.ds(0, bits_hbm.shape[0]), :], load_sem.at[2]),
        pltpu.make_async_copy(w_hbm.at[0], w_ref, load_sem.at[3]),
        pltpu.make_async_copy(damp_hbm, damp_ref, load_sem.at[4]),
    ]
    barrier = pltpu.get_barrier_semaphore()
    for device in (to_mate, to_x, to_core, to_y):
        pl.semaphore_signal(barrier, inc=1, device_id=device, device_id_type=MESH)

    @pl.when(inner == 1)
    def _():
        pl.semaphore_signal(barrier, inc=1, device_id=to_across, device_id_type=MESH)

    for load in loads:
        load.start()

    def block(number, h, sem, device):
        lo, size = spans[h]
        piece = held.at[number, :, pl.ds(lo, size)]
        return pltpu.make_async_remote_copy(
            src_ref=piece, dst_ref=piece, send_sem=sem, recv_sem=recv_sem.at[number, h],
            device_id=device, device_id_type=MESH)

    def arrived(number, h):
        block(number, h, x_sem.at[0, 0], to_x).wait_recv()

    always, inners = [], []

    def send(number, h, sem, device):
        copy = block(number, h, sem, device)
        copy.start()
        always.append(copy)

    def inward(number, h, sem, device):
        @pl.when(inner == 1)
        def _():
            block(number, h, sem, device).start()

        inners.append(block(number, h, sem, device))

    def spread(number, h):
        inward(number, h, across_sem.at[0, h], to_across)
        send(number, h, mate_sem.at[0, h], to_mate)
        send(number, h, x_sem.at[0, h], to_x)
        send(number, h, core_sem.at[0, h], to_core)

    def column(step, h):
        number = order[step] * 4 + cross
        arrived(number, h)
        if step == 1:
            inward(number, h, across_sem.at[1, h], to_across)
        else:
            inward(number, h, mate_sem.at[step, h], to_mate)
        if not (step == 1 and h == 1):
            send(number, h, x_sem.at[step, h], to_x)
        send(number, h, core_sem.at[step, h], to_core)

    def crossed(step):
        number = order[step] * 4 + x_row
        for h in (0, 1):
            arrived(number, h)
            send(number, h, core_sem.at[4 + step, h], to_core)

    def around():
        send(z * 4 + x_row, 1, mate_sem.at[1, 0], to_mate)

    def rows_of(first, count):
        return pl.ds(pl.multiple_of(first * tok_count, tok_count), count * tok_count)

    def y_copy(first, count, which):
        rows = rows_of(first, count)
        return pltpu.make_async_remote_copy(
            src_ref=part.at[rows, :], dst_ref=other.at[rows, :], send_sem=y_send.at[which],
            recv_sem=y_recv.at[which], device_id=to_y, device_id_type=MESH)

    def member(flags):
        lane = lax.broadcasted_iota(jnp.int32, flags.shape, 1)
        return jnp.sum(jnp.where(lane == mine, flags.astype(jnp.float32), 0.0), axis=1, keepdims=True)

    summed = []

    def project(first, count):
        rows, blocks = count * tok_count, pl.ds(first, count)
        tokens = held[blocks, :, 0:feat].reshape(rows, feat)
        part[rows_of(first, count), :] = lax.dot_general(
            pruned[...], tokens, (((1,), (1,)), ((), ())), preferred_element_type=jnp.float32).T
        copy = y_copy(first, count, len(summed))
        copy.start()
        summed.append(copy)
        here = member(held[blocks, :, feat:feat + FLAGS].reshape(rows, FLAGS))
        for lo in range(0, feat, CHUNK):
            piece = held[blocks, :, lo:lo + CHUNK].reshape(rows, CHUNK).astype(jnp.float32)
            total = jnp.sum((piece * piece * here).reshape(-1, 8, CHUNK), axis=0)
            squares[:, lo:lo + CHUNK] = total if len(summed) == 1 else squares[:, lo:lo + CHUNK] + total

    def other_core(step, row):
        for h in (0, 1):
            arrived(order[step] * 4 + row, h)

    def plane(step):
        other_core(step, core_row)
        other_core(step, both_row)
        project(order[step] * 4, 4)

    loads[1].wait()
    wide_ids[...] = jnp.full_like(wide_ids, -1)
    wide_ids[:, 0:tok_count] = ids_ref[...]
    expert = lax.broadcasted_iota(jnp.int32, (FLAGS, 128), 0)
    named = jnp.zeros((FLAGS, 128), jnp.float32)
    for k in range(ids_ref.shape[0]):
        named = jnp.where(wide_ids[k:k + 1, :] == expert, 1.0, named)
    held[mine, :, feat:feat + FLAGS] = named.T[0:tok_count, :].astype(jnp.bfloat16)
    loads[0].wait()
    pl.semaphore_wait(barrier, 4 + inner)

    for h in (0, 1):
        spread(mine, h)

    filled = bits_hbm.shape[0]
    if filled < 128:
        bits_ref[filled:128, :] = jnp.zeros((128 - filled, slab), jnp.int32)
    loads[2].wait()
    loads[3].wait()
    words[...] = bits_ref[...].T

    spot = lax.broadcasted_iota(jnp.int32, (1, 128), 1)
    group = jnp.right_shift(spot, 5)
    probe = jnp.left_shift(jnp.int32(1), jnp.bitwise_and(spot, 31))

    def unpack(j, carry):
        at = pl.ds(pl.multiple_of(j * 128, 128), 128)
        index = jnp.broadcast_to(group + 4 * j, (slab, 128))
        word = jnp.take_along_axis(words[...], index, axis=1)
        flag = jnp.where(jnp.bitwise_and(word, probe) != 0, 1.0, 0.0).astype(jnp.bfloat16)
        keep[:, at] = flag
        pruned[:, at] = w_ref[:, at] * (jnp.bfloat16(1.0) - flag)
        return carry

    steps = feat // 128
    lax.fori_loop(0, steps, unpack, 0)
    for h in (0, 1):
        column(1, h)
        column(2, h)
    crossed(0)
    column(3, 0)
    column(3, 1)
    around()
    crossed(2)
    plane(0)
    crossed(1)
    plane(2)
    crossed(3)
    plane(1)
    other_core(3, core_row)
    project(order[3] * 4 + 2 * x, 2)
    other_core(3, both_row)
    project(order[3] * 4 + 2 * (1 - x), 2)

    loads[4].wait()
    here = member(held[:, :, feat:feat + FLAGS].reshape(-1, FLAGS))
    for copy in summed:
        copy.wait_recv()
    projected = jnp.where(here > 0.5, part[...] + other[...], 0.0).T.astype(jnp.bfloat16)
    stores = []
    for lo in range(0, feat, WIDE):
        at = slice(lo, lo + WIDE)
        routed = held[:, :, at].reshape(-1, WIDE)
        comp = jnp.dot(projected, routed, preferred_element_type=jnp.float32)
        diag = jnp.sum(squares[:, at], axis=0, keepdims=True) / ROWS_E + damp_ref[:, at]
        updated = w_ref[:, at].astype(jnp.float32) + comp * (ETA / ROWS_E / diag)
        out_ref[:, at] = updated.astype(jnp.bfloat16) * keep[:, at]
        store = pltpu.make_async_copy(out_ref.at[:, at], out_hbm.at[0, :, at], store_sem.at[lo // WIDE])
        store.start()
        stores.append(store)

    for copy in always:
        copy.wait_send()
    for copy in summed:
        copy.wait_send()

    @pl.when(inner == 1)
    def _():
        for copy in inners:
            copy.wait_send()

    for store in stores:
        store.wait()


def leave(from_hbm, to_hbm, sems):
    rows = from_hbm.shape[1] // 4
    copies = []
    for i in range(4):
        at = pl.ds(i * rows, rows)
        copies.append(pltpu.make_async_copy(from_hbm.at[0, at, :], to_hbm.at[0, at, :], sems.at[i]))
    for copy in copies:
        copy.start()
    for copy in copies:
        copy.wait()


def gathered(tokens, expert_ids, weight, mask_bits, damping):
    tok_count, feat = tokens.shape
    slab = weight.shape[1]
    blocks = 16
    total = blocks * tok_count
    dma = pltpu.SemaphoreType.DMA
    result = pl.pallas_call(
        kernel,
        out_shape=jax.ShapeDtypeStruct(weight.shape, jnp.bfloat16),
        in_specs=[pl.BlockSpec(memory_space=pltpu.HBM)] * 5,
        out_specs=pl.BlockSpec(memory_space=pl.ANY),
        scratch_shapes=[
            pltpu.VMEM((blocks, tok_count, feat + FLAGS), jnp.bfloat16),
            pltpu.VMEM((slab, feat), jnp.bfloat16),
            pltpu.VMEM((slab, feat), jnp.bfloat16),
            pltpu.VMEM((slab, feat), jnp.bfloat16),
            pltpu.VMEM((total, slab), jnp.float32),
            pltpu.VMEM((total, slab), jnp.float32),
            pltpu.VMEM((8, feat), jnp.float32),
            pltpu.VMEM((expert_ids.shape[1], tok_count), jnp.int32),
            pltpu.VMEM((expert_ids.shape[1], 128), jnp.int32),
            pltpu.VMEM((128, slab), jnp.int32),
            pltpu.VMEM((slab, 128), jnp.int32),
            pltpu.VMEM((1, feat), jnp.float32),
            pltpu.VMEM((slab, feat), jnp.bfloat16),
            dma((5,)),
            dma((blocks, 2)),
            dma((4, 2)),
            dma((8, 2)),
            dma((4, 2)),
            dma((2, 2)),
            dma((5,)),
            dma((5,)),
            dma((feat // WIDE,)),
        ],
        compiler_params=pltpu.CompilerParams(
            collective_id=0, has_side_effects=True, vmem_limit_bytes=62 * 1024 * 1024),
        cost_estimate=pl.CostEstimate(
            flops=4 * total * slab * feat, bytes_accessed=4 * slab * feat, transcendentals=0),
    )(tokens, expert_ids.T, weight, mask_bits.T, damping)
    return pl.pallas_call(
        leave,
        out_shape=jax.ShapeDtypeStruct(weight.shape, jnp.bfloat16),
        in_specs=[pl.BlockSpec(memory_space=pl.ANY)],
        out_specs=pl.BlockSpec(memory_space=pl.ANY),
        scratch_shapes=[dma((4,))],
    )(result)


def solution(mesh):
    in_specs = (
        P(("expert", "hrow"), "hcol"),
        P(("expert", "hrow"), None),
        P(("expert", "hrow"), None, "hcol"),
        P(None, "hcol"),
        P(("expert", "hrow"), "hcol"),
    )
    out_specs = P(("expert", "hrow"), None, "hcol")
    line, cross = mesh.shape["expert"], mesh.shape["hrow"]

    def body(tokens, expert_ids, weight, mask_bits, damping):
        tok_count, top_count = expert_ids.shape
        capacity = 2 * tok_count * top_count // (line * cross * weight.shape[0])
        fits = line == 4 and cross == 4 and mesh.shape["hcol"] == 2 and weight.shape[0] == 1
        if fits and capacity >= tok_count:
            return gathered(tokens, expert_ids, weight, mask_bits, damping)
        return local(tokens, expert_ids, weight, mask_bits, damping)

    return jax.shard_map(body, mesh=mesh, in_specs=in_specs, out_specs=out_specs, check_vma=False)
```

```python
import functools

import jax
import jax.numpy as jnp
from jax import lax
from jax.experimental import pallas as pl
from jax.experimental.pallas import tpu as pltpu
from jax.sharding import PartitionSpec as P

ROWS_E = 128


ETA = 0.5


def unpack_bits(bits):
    bit_shifts = jnp.arange(32, dtype=jnp.int32)
    bit_flags = jnp.bitwise_and(jnp.right_shift(bits[:, :, None], bit_shifts[None, None, :]), 1)
    return bit_flags.reshape(bits.shape[0], bits.shape[1] * 32)


def route_rows(tokens, expert_ids, group_count, local_count):
    tok_count, top_count = expert_ids.shape
    expert_count = group_count * local_count
    capacity = 2 * tok_count * top_count // expert_count
    flat_ids = expert_ids.reshape(-1)
    one_hot = (flat_ids[:, None] == jnp.arange(expert_count, dtype=jnp.int32)[None, :]).astype(
        jnp.int32
    )
    prior_count = jnp.cumsum(one_hot, axis=0) - one_hot
    slot_index = jnp.sum(prior_count * one_hot, axis=1)
    group_of = flat_ids // local_count
    local_of = flat_ids % local_count
    target_slot = ((local_of * group_count + group_of) * capacity + slot_index).reshape(
        tok_count, top_count
    )
    slot_ids = jnp.arange(expert_count * capacity, dtype=jnp.int32)
    selector = jnp.any(slot_ids[:, None, None] == target_slot[None, :, :], axis=2).astype(
        jnp.bfloat16
    )
    packed = jnp.dot(selector, tokens, preferred_element_type=jnp.float32).astype(jnp.bfloat16)
    return packed.reshape(local_count, group_count, 1, capacity, tokens.shape[1])


def local(tokens, expert_ids, weight, mask_bits, damping):
    group_count = lax.axis_size(("expert", "hrow"))
    local_experts = weight.shape[0]
    feat_width = tokens.shape[1]
    slab_rows = weight.shape[1]
    packed = route_rows(tokens, expert_ids, group_count, local_experts)
    keep_flags = unpack_bits(mask_bits)
    keep_mask = keep_flags[None, :, :] == 1
    pruned = jnp.where(keep_mask, jnp.zeros_like(weight), weight)
    block = lax.all_to_all(packed, ("expert", "hrow"), split_axis=1, concat_axis=2, tiled=True)
    partials = jnp.einsum("esf,exgcf->exgcs", pruned, block, preferred_element_type=jnp.float32)
    slot_count = block.shape[1] * block.shape[2] * block.shape[3]
    routed = block.reshape(local_experts, slot_count, feat_width)
    partials = partials.reshape(local_experts, slot_count, slab_rows)
    projected = lax.psum(partials, "hcol").astype(jnp.bfloat16)
    comp_term = (
        jnp.einsum("ers,erf->esf", projected, routed, preferred_element_type=jnp.float32) / ROWS_E
    )
    diag_scale = (
        jnp.einsum("erf,erf->ef", routed, routed, preferred_element_type=jnp.float32) / ROWS_E
        + damping
    )
    updated = weight.astype(jnp.float32) + ETA * comp_term / diag_scale[:, None, :]
    return jnp.where(keep_mask, updated, jnp.float32(0.0)).astype(jnp.bfloat16)


MESH = pl.DeviceIdType.MESH
FLAGS = 128
CHUNK = 256
WIDE = 512
PIECES = 4


def kernel(tok_hbm, ids_hbm, w_hbm, bits_hbm, damp_hbm, out_hbm,
           held, w_ref, pruned, keep, part, other, squares, ids_ref, wide_ids, bits_ref, words, damp_ref, out_ref,
           load_sem, recv_sem, x_sem, core_sem, mate_sem, across_sem, y_send, y_recv, store_sem):
    z, cross, y = lax.axis_index("expert"), lax.axis_index("hrow"), lax.axis_index("hcol")
    tok_count, feat = tok_hbm.shape
    slab = w_hbm.shape[1]
    quarter = feat // (128 * PIECES) * 128
    spans = [(i * quarter, quarter) for i in range(PIECES - 1)]
    spans.append(((PIECES - 1) * quarter, feat + FLAGS - (PIECES - 1) * quarter))
    whole = (0, feat + FLAGS)
    x, core = cross // 2, cross % 2
    upper = z // 2
    inner = (z + 1) // 2 % 2
    mate = 4 * upper + 1 - z
    across = 3 - z
    order = (z, mate, 2 - upper, 3 - 3 * upper)
    x_row, core_row = (1 - x) * 2 + core, x * 2 + 1 - core
    both_row = (1 - x) * 2 + 1 - core
    to_mate, to_across = (mate, cross, y), (across, cross, y)
    to_x, to_core, to_y = (z, x_row, y), (z, core_row, y), (z, cross, 1 - y)
    mine = z * 4 + cross

    loads = [
        pltpu.make_async_copy(tok_hbm, held.at[mine, :, pl.ds(0, feat)], load_sem.at[0]),
        pltpu.make_async_copy(ids_hbm, ids_ref, load_sem.at[1]),
        pltpu.make_async_copy(bits_hbm, bits_ref.at[pl.ds(0, bits_hbm.shape[0]), :], load_sem.at[2]),
        pltpu.make_async_copy(w_hbm.at[0], w_ref, load_sem.at[3]),
        pltpu.make_async_copy(damp_hbm, damp_ref, load_sem.at[4]),
    ]
    barrier = pltpu.get_barrier_semaphore()
    for device in (to_mate, to_x, to_core, to_y):
        pl.semaphore_signal(barrier, inc=1, device_id=device, device_id_type=MESH)

    @pl.when(inner == 1)
    def _():
        pl.semaphore_signal(barrier, inc=1, device_id=to_across, device_id_type=MESH)

    for load in loads:
        load.start()

    def block(number, h, sem, device):
        lo, size = whole if h is None else spans[h]
        piece = held.at[number, :, pl.ds(lo, size)]
        return pltpu.make_async_remote_copy(
            src_ref=piece, dst_ref=piece, send_sem=sem, recv_sem=recv_sem.at[number, h or 0],
            device_id=device, device_id_type=MESH)

    def arrived(number, h):
        block(number, h, x_sem.at[0, 0], to_x).wait_recv()

    always, inners = [], []

    def send(number, h, sem, device):
        copy = block(number, h, sem, device)
        copy.start()
        always.append(copy)

    def inward(number, h, sem, device):
        @pl.when(inner == 1)
        def _():
            block(number, h, sem, device).start()

        inners.append(block(number, h, sem, device))

    def spread(number, h):
        inward(number, h, across_sem.at[0, h], to_across)
        send(number, h, mate_sem.at[0, h], to_mate)
        send(number, h, x_sem.at[0, h], to_x)

    def column(step, h):
        number = order[step] * 4 + cross
        arrived(number, h)
        if step == 1:
            inward(number, h, across_sem.at[1, h], to_across)
        else:
            inward(number, h, mate_sem.at[step, h], to_mate)
        send(number, h, x_sem.at[step, h], to_x)

    def to_other_core(step):
        send(order[step] * 4 + cross, None, core_sem.at[step], to_core)

    def crossed(step):
        number = order[step] * 4 + x_row
        for h in range(PIECES):
            arrived(number, h)
        send(number, None, core_sem.at[4 + step], to_core)

    def rows_of(first, count):
        return pl.ds(pl.multiple_of(first * tok_count, tok_count), count * tok_count)

    def y_copy(first, count, which):
        rows = rows_of(first, count)
        return pltpu.make_async_remote_copy(
            src_ref=part.at[rows, :], dst_ref=other.at[rows, :], send_sem=y_send.at[which],
            recv_sem=y_recv.at[which], device_id=to_y, device_id_type=MESH)

    def member(flags):
        lane = lax.broadcasted_iota(jnp.int32, flags.shape, 1)
        return jnp.sum(jnp.where(lane == mine, flags.astype(jnp.float32), 0.0), axis=1, keepdims=True)

    summed = []

    def project(first, count):
        rows, blocks = count * tok_count, pl.ds(first, count)
        tokens = held[blocks, :, 0:feat].reshape(rows, feat)
        part[rows_of(first, count), :] = lax.dot_general(
            pruned[...], tokens, (((1,), (1,)), ((), ())), preferred_element_type=jnp.float32).T
        copy = y_copy(first, count, len(summed))
        copy.start()
        summed.append(copy)
        here = member(held[blocks, :, feat:feat + FLAGS].reshape(rows, FLAGS))
        for lo in range(0, feat, CHUNK):
            piece = held[blocks, :, lo:lo + CHUNK].reshape(rows, CHUNK).astype(jnp.float32)
            total = jnp.sum((piece * piece * here).reshape(-1, 8, CHUNK), axis=0)
            squares[:, lo:lo + CHUNK] = total if len(summed) == 1 else squares[:, lo:lo + CHUNK] + total

    def other_core(step, row):
        arrived(order[step] * 4 + row, None)

    def plane(step):
        other_core(step, core_row)
        other_core(step, both_row)
        project(order[step] * 4, 4)

    loads[1].wait()
    wide_ids[...] = jnp.full_like(wide_ids, -1)
    wide_ids[:, 0:tok_count] = ids_ref[...]
    expert = lax.broadcasted_iota(jnp.int32, (FLAGS, 128), 0)
    named = jnp.zeros((FLAGS, 128), jnp.float32)
    for k in range(ids_ref.shape[0]):
        named = jnp.where(wide_ids[k:k + 1, :] == expert, 1.0, named)
    held[mine, :, feat:feat + FLAGS] = named.T[0:tok_count, :].astype(jnp.bfloat16)
    loads[0].wait()
    pl.semaphore_wait(barrier, 4 + inner)

    for h in range(PIECES):
        spread(mine, h)
    to_other_core(0)

    filled = bits_hbm.shape[0]
    if filled < 128:
        bits_ref[filled:128, :] = jnp.zeros((128 - filled, slab), jnp.int32)
    loads[2].wait()
    loads[3].wait()
    words[...] = bits_ref[...].T

    spot = lax.broadcasted_iota(jnp.int32, (1, 128), 1)
    group = jnp.right_shift(spot, 5)
    probe = jnp.left_shift(jnp.int32(1), jnp.bitwise_and(spot, 31))

    def unpack(j, carry):
        at = pl.ds(pl.multiple_of(j * 128, 128), 128)
        index = jnp.broadcast_to(group + 4 * j, (slab, 128))
        word = jnp.take_along_axis(words[...], index, axis=1)
        flag = jnp.where(jnp.bitwise_and(word, probe) != 0, 1.0, 0.0).astype(jnp.bfloat16)
        keep[:, at] = flag
        pruned[:, at] = w_ref[:, at] * (jnp.bfloat16(1.0) - flag)
        return carry

    steps = feat // 128
    lax.fori_loop(0, steps, unpack, 0)
    for h in range(PIECES):
        column(1, h)
        column(2, h)
    to_other_core(1)
    to_other_core(2)
    crossed(0)
    for h in range(PIECES):
        column(3, h)
    to_other_core(3)
    crossed(1)
    crossed(2)
    plane(0)
    plane(1)
    crossed(3)
    plane(2)
    other_core(3, core_row)
    project(order[3] * 4 + 2 * x, 2)
    other_core(3, both_row)
    project(order[3] * 4 + 2 * (1 - x), 2)

    loads[4].wait()
    here = member(held[:, :, feat:feat + FLAGS].reshape(-1, FLAGS))
    for copy in summed:
        copy.wait_recv()
    projected = jnp.where(here > 0.5, part[...] + other[...], 0.0).T.astype(jnp.bfloat16)
    stores = []
    for lo in range(0, feat, WIDE):
        at = slice(lo, lo + WIDE)
        routed = held[:, :, at].reshape(-1, WIDE)
        comp = jnp.dot(projected, routed, preferred_element_type=jnp.float32)
        diag = jnp.sum(squares[:, at], axis=0, keepdims=True) / ROWS_E + damp_ref[:, at]
        updated = w_ref[:, at].astype(jnp.float32) + comp * (ETA / ROWS_E / diag)
        out_ref[:, at] = updated.astype(jnp.bfloat16) * keep[:, at]
        store = pltpu.make_async_copy(out_ref.at[:, at], out_hbm.at[0, :, at], store_sem.at[lo // WIDE])
        store.start()
        stores.append(store)

    for copy in always:
        copy.wait_send()
    for copy in summed:
        copy.wait_send()

    @pl.when(inner == 1)
    def _():
        for copy in inners:
            copy.wait_send()

    for store in stores:
        store.wait()


def leave(from_hbm, to_hbm, slabs, in_sems, out_sems):
    count, rows = slabs.shape[0], slabs.shape[1]
    ins, outs = [], []
    for i in range(count):
        at = pl.ds(i * rows, rows)
        ins.append(pltpu.make_async_copy(from_hbm.at[0, at, :], slabs.at[i], in_sems.at[i]))
        outs.append(pltpu.make_async_copy(slabs.at[i], to_hbm.at[0, at, :], out_sems.at[i]))
        ins[i].start()
    for i in range(count):
        ins[i].wait()
        outs[i].start()
    for out in outs:
        out.wait()


def gathered(tokens, expert_ids, weight, mask_bits, damping):
    tok_count, feat = tokens.shape
    slab = weight.shape[1]
    blocks = 16
    total = blocks * tok_count
    dma = pltpu.SemaphoreType.DMA
    result = pl.pallas_call(
        kernel,
        out_shape=jax.ShapeDtypeStruct(weight.shape, jnp.bfloat16),
        in_specs=[pl.BlockSpec(memory_space=pltpu.HBM)] * 5,
        out_specs=pl.BlockSpec(memory_space=pl.ANY),
        scratch_shapes=[
            pltpu.VMEM((blocks, tok_count, feat + FLAGS), jnp.bfloat16),
            pltpu.VMEM((slab, feat), jnp.bfloat16),
            pltpu.VMEM((slab, feat), jnp.bfloat16),
            pltpu.VMEM((slab, feat), jnp.bfloat16),
            pltpu.VMEM((total, slab), jnp.float32),
            pltpu.VMEM((total, slab), jnp.float32),
            pltpu.VMEM((8, feat), jnp.float32),
            pltpu.VMEM((expert_ids.shape[1], tok_count), jnp.int32),
            pltpu.VMEM((expert_ids.shape[1], 128), jnp.int32),
            pltpu.VMEM((128, slab), jnp.int32),
            pltpu.VMEM((slab, 128), jnp.int32),
            pltpu.VMEM((1, feat), jnp.float32),
            pltpu.VMEM((slab, feat), jnp.bfloat16),
            dma((5,)),
            dma((blocks, PIECES)),
            dma((4, PIECES)),
            dma((8,)),
            dma((4, PIECES)),
            dma((2, PIECES)),
            dma((5,)),
            dma((5,)),
            dma((feat // WIDE,)),
        ],
        compiler_params=pltpu.CompilerParams(
            collective_id=0, has_side_effects=True, vmem_limit_bytes=62 * 1024 * 1024),
        cost_estimate=pl.CostEstimate(
            flops=4 * total * slab * feat, bytes_accessed=4 * slab * feat, transcendentals=0),
    )(tokens, expert_ids.T, weight, mask_bits.T, damping)
    return pl.pallas_call(
        leave,
        out_shape=jax.ShapeDtypeStruct(weight.shape, jnp.bfloat16),
        in_specs=[pl.BlockSpec(memory_space=pl.ANY)],
        out_specs=pl.BlockSpec(memory_space=pl.ANY),
        scratch_shapes=[pltpu.VMEM((8, slab // 8, feat), jnp.bfloat16), dma((8,)), dma((8,))],
        compiler_params=pltpu.CompilerParams(vmem_limit_bytes=62 * 1024 * 1024),
    )(result)


def solution(mesh):
    in_specs = (
        P(("expert", "hrow"), "hcol"),
        P(("expert", "hrow"), None),
        P(("expert", "hrow"), None, "hcol"),
        P(None, "hcol"),
        P(("expert", "hrow"), "hcol"),
    )
    out_specs = P(("expert", "hrow"), None, "hcol")
    line, cross = mesh.shape["expert"], mesh.shape["hrow"]

    def body(tokens, expert_ids, weight, mask_bits, damping):
        tok_count, top_count = expert_ids.shape
        capacity = 2 * tok_count * top_count // (line * cross * weight.shape[0])
        fits = line == 4 and cross == 4 and mesh.shape["hcol"] == 2 and weight.shape[0] == 1
        if fits and capacity >= tok_count:
            return gathered(tokens, expert_ids, weight, mask_bits, damping)
        return local(tokens, expert_ids, weight, mask_bits, damping)

    return jax.shard_map(body, mesh=mesh, in_specs=in_specs, out_specs=out_specs, check_vma=False)
```

```python
import functools

import jax
import jax.numpy as jnp
from jax import lax
from jax.experimental import pallas as pl
from jax.experimental.pallas import tpu as pltpu
from jax.sharding import PartitionSpec as P

ROWS_E = 128


ETA = 0.5


def unpack_bits(bits):
    bit_shifts = jnp.arange(32, dtype=jnp.int32)
    bit_flags = jnp.bitwise_and(jnp.right_shift(bits[:, :, None], bit_shifts[None, None, :]), 1)
    return bit_flags.reshape(bits.shape[0], bits.shape[1] * 32)


def route_rows(tokens, expert_ids, group_count, local_count):
    tok_count, top_count = expert_ids.shape
    expert_count = group_count * local_count
    capacity = 2 * tok_count * top_count // expert_count
    flat_ids = expert_ids.reshape(-1)
    one_hot = (flat_ids[:, None] == jnp.arange(expert_count, dtype=jnp.int32)[None, :]).astype(
        jnp.int32
    )
    prior_count = jnp.cumsum(one_hot, axis=0) - one_hot
    slot_index = jnp.sum(prior_count * one_hot, axis=1)
    group_of = flat_ids // local_count
    local_of = flat_ids % local_count
    target_slot = ((local_of * group_count + group_of) * capacity + slot_index).reshape(
        tok_count, top_count
    )
    slot_ids = jnp.arange(expert_count * capacity, dtype=jnp.int32)
    selector = jnp.any(slot_ids[:, None, None] == target_slot[None, :, :], axis=2).astype(
        jnp.bfloat16
    )
    packed = jnp.dot(selector, tokens, preferred_element_type=jnp.float32).astype(jnp.bfloat16)
    return packed.reshape(local_count, group_count, 1, capacity, tokens.shape[1])


def local(tokens, expert_ids, weight, mask_bits, damping):
    group_count = lax.axis_size(("expert", "hrow"))
    local_experts = weight.shape[0]
    feat_width = tokens.shape[1]
    slab_rows = weight.shape[1]
    packed = route_rows(tokens, expert_ids, group_count, local_experts)
    keep_flags = unpack_bits(mask_bits)
    keep_mask = keep_flags[None, :, :] == 1
    pruned = jnp.where(keep_mask, jnp.zeros_like(weight), weight)
    block = lax.all_to_all(packed, ("expert", "hrow"), split_axis=1, concat_axis=2, tiled=True)
    partials = jnp.einsum("esf,exgcf->exgcs", pruned, block, preferred_element_type=jnp.float32)
    slot_count = block.shape[1] * block.shape[2] * block.shape[3]
    routed = block.reshape(local_experts, slot_count, feat_width)
    partials = partials.reshape(local_experts, slot_count, slab_rows)
    projected = lax.psum(partials, "hcol").astype(jnp.bfloat16)
    comp_term = (
        jnp.einsum("ers,erf->esf", projected, routed, preferred_element_type=jnp.float32) / ROWS_E
    )
    diag_scale = (
        jnp.einsum("erf,erf->ef", routed, routed, preferred_element_type=jnp.float32) / ROWS_E
        + damping
    )
    updated = weight.astype(jnp.float32) + ETA * comp_term / diag_scale[:, None, :]
    return jnp.where(keep_mask, updated, jnp.float32(0.0)).astype(jnp.bfloat16)


MESH = pl.DeviceIdType.MESH
FLAGS = 128
CHUNK = 256
WIDE = 512
PIECES = 4


def kernel(tok_hbm, ids_hbm, w_hbm, bits_hbm, damp_hbm, out_hbm,
           held, w_ref, pruned, keep, part, other, squares, ids_ref, wide_ids, bits_ref, words, damp_ref, out_ref,
           load_sem, recv_sem, x_sem, core_sem, mate_sem, across_sem, y_send, y_recv, store_sem):
    z, cross, y = lax.axis_index("expert"), lax.axis_index("hrow"), lax.axis_index("hcol")
    tok_count, feat = tok_hbm.shape
    slab = w_hbm.shape[1]
    quarter = feat // (128 * PIECES) * 128
    spans = [(i * quarter, quarter) for i in range(PIECES - 1)]
    spans.append(((PIECES - 1) * quarter, feat + FLAGS - (PIECES - 1) * quarter))
    whole = (0, feat + FLAGS)
    x, core = cross // 2, cross % 2
    upper = z // 2
    inner = (z + 1) // 2 % 2
    mate = 4 * upper + 1 - z
    across = 3 - z
    order = (z, mate, 2 - upper, 3 - 3 * upper)
    x_row, core_row = (1 - x) * 2 + core, x * 2 + 1 - core
    both_row = (1 - x) * 2 + 1 - core
    to_mate, to_across = (mate, cross, y), (across, cross, y)
    to_x, to_core, to_y = (z, x_row, y), (z, core_row, y), (z, cross, 1 - y)
    mine = z * 4 + cross

    loads = [
        pltpu.make_async_copy(tok_hbm, held.at[mine, :, pl.ds(0, feat)], load_sem.at[0]),
        pltpu.make_async_copy(ids_hbm, ids_ref, load_sem.at[1]),
        pltpu.make_async_copy(bits_hbm, bits_ref.at[pl.ds(0, bits_hbm.shape[0]), :], load_sem.at[2]),
        pltpu.make_async_copy(w_hbm.at[0], w_ref, load_sem.at[3]),
        pltpu.make_async_copy(damp_hbm, damp_ref, load_sem.at[4]),
    ]
    barrier = pltpu.get_barrier_semaphore()
    for device in (to_mate, to_x, to_core, to_y):
        pl.semaphore_signal(barrier, inc=1, device_id=device, device_id_type=MESH)

    @pl.when(inner == 1)
    def _():
        pl.semaphore_signal(barrier, inc=1, device_id=to_across, device_id_type=MESH)

    for load in loads:
        load.start()

    def block(number, h, sem, device):
        lo, size = whole if h is None else spans[h]
        piece = held.at[number, :, pl.ds(lo, size)]
        return pltpu.make_async_remote_copy(
            src_ref=piece, dst_ref=piece, send_sem=sem, recv_sem=recv_sem.at[number, h or 0],
            device_id=device, device_id_type=MESH)

    def arrived(number, h):
        block(number, h, x_sem.at[0, 0], to_x).wait_recv()

    sent = {None: [], 0: [], 1: []}
    own_column = [order[step] * 4 + cross for step in range(4)]
    other_column = [order[step] * 4 + x_row for step in range(4)]

    def send(number, h, sem, at, device, where=None):
        block(number, h, sem.at[at], device).start()
        sent[where].append((number, h, sem, at, device))

    def send_on(kind, number, h, sem, at, device):
        @pl.when(inner == kind)
        def _():
            send(number, h, sem, at, device, kind)

    def finish(where):
        for number, h, sem, at, device in sent[where]:
            block(number, h, sem.at[at], device).wait_send()

    def spread(h):
        send_on(1, mine, h, across_sem, (0, h), to_across)
        send(mine, h, mate_sem, (0, h), to_mate)
        send(mine, h, x_sem, (0, h), to_x)

    def column(step, h, where=None):
        number = own_column[step]
        arrived(number, h)
        if where != 0:
            sem, device = (across_sem, to_across) if step == 1 else (mate_sem, to_mate)
            at = (1, h) if step == 1 else (step, h)
            if where == 1:
                send(number, h, sem, at, device, 1)
            else:
                send_on(1, number, h, sem, at, device)
        if step > 1 or (where == 0 and h < PIECES // 2):
            send(number, h, x_sem, (step, h), to_x, where)

    def to_other_core(step):
        send(own_column[step], None, core_sem, (step, 0), to_core)

    def crossed(step):
        for h in range(PIECES):
            arrived(other_column[step], h)
            if step == 3:
                send(other_column[step], h, core_sem, (4 + step, h), to_core)
        if step < 3:
            send(other_column[step], None, core_sem, (4 + step, 0), to_core)

    def rows_of(first, count):
        return pl.ds(pl.multiple_of(first * tok_count, tok_count), count * tok_count)

    def y_copy(first, count, which):
        rows = rows_of(first, count)
        return pltpu.make_async_remote_copy(
            src_ref=part.at[rows, :], dst_ref=other.at[rows, :], send_sem=y_send.at[which],
            recv_sem=y_recv.at[which], device_id=to_y, device_id_type=MESH)

    def member(flags):
        lane = lax.broadcasted_iota(jnp.int32, flags.shape, 1)
        return jnp.sum(jnp.where(lane == mine, flags.astype(jnp.float32), 0.0), axis=1, keepdims=True)

    summed = []

    def project(first, count):
        rows, blocks = count * tok_count, pl.ds(first, count)
        tokens = held[blocks, :, 0:feat].reshape(rows, feat)
        part[rows_of(first, count), :] = lax.dot_general(
            pruned[...], tokens, (((1,), (1,)), ((), ())), preferred_element_type=jnp.float32).T
        copy = y_copy(first, count, len(summed))
        copy.start()
        summed.append(copy)
        here = member(held[blocks, :, feat:feat + FLAGS].reshape(rows, FLAGS))
        for lo in range(0, feat, CHUNK):
            piece = held[blocks, :, lo:lo + CHUNK].reshape(rows, CHUNK).astype(jnp.float32)
            total = jnp.sum((piece * piece * here).reshape(-1, 8, CHUNK), axis=0)
            squares[:, lo:lo + CHUNK] = total if len(summed) == 1 else squares[:, lo:lo + CHUNK] + total

    def other_core(step, row):
        for h in range(PIECES) if step == 3 and row is both_row else (None,):
            arrived(order[step] * 4 + row, h)

    def plane(step):
        other_core(step, core_row)
        other_core(step, both_row)
        project(order[step] * 4, 4)

    loads[1].wait()
    wide_ids[...] = jnp.full_like(wide_ids, -1)
    wide_ids[:, 0:tok_count] = ids_ref[...]
    expert = lax.broadcasted_iota(jnp.int32, (FLAGS, 128), 0)
    named = jnp.zeros((FLAGS, 128), jnp.float32)
    for k in range(ids_ref.shape[0]):
        named = jnp.where(wide_ids[k:k + 1, :] == expert, 1.0, named)
    held[mine, :, feat:feat + FLAGS] = named.T[0:tok_count, :].astype(jnp.bfloat16)
    loads[0].wait()
    pl.semaphore_wait(barrier, 4 + inner)

    for h in range(PIECES):
        spread(h)
    to_other_core(0)

    filled = bits_hbm.shape[0]
    if filled < 128:
        bits_ref[filled:128, :] = jnp.zeros((128 - filled, slab), jnp.int32)
    loads[2].wait()
    loads[3].wait()
    words[...] = bits_ref[...].T

    spot = lax.broadcasted_iota(jnp.int32, (1, 128), 1)
    group = jnp.right_shift(spot, 5)
    probe = jnp.left_shift(jnp.int32(1), jnp.bitwise_and(spot, 31))

    def unpack(j, carry):
        at = pl.ds(pl.multiple_of(j * 128, 128), 128)
        index = jnp.broadcast_to(group + 4 * j, (slab, 128))
        word = jnp.take_along_axis(words[...], index, axis=1)
        flag = jnp.where(jnp.bitwise_and(word, probe) != 0, 1.0, 0.0).astype(jnp.bfloat16)
        keep[:, at] = flag
        pruned[:, at] = w_ref[:, at] * (jnp.bfloat16(1.0) - flag)
        return carry

    steps = feat // 128
    lax.fori_loop(0, steps, unpack, 0)
    @pl.when(inner == 1)
    def _():
        for h in range(PIECES):
            column(1, h, 1)
            column(2, h, 1)
        for h in range(PIECES):
            arrived(other_column[0], h)

    @pl.when(inner == 0)
    def _():
        for h in range(PIECES):
            column(1, h, 0)
            arrived(other_column[0], h)
            send(other_column[0], h, mate_sem, (1, h), to_mate, 0)
        for h in range(PIECES):
            column(2, h, 0)

    to_other_core(1)
    to_other_core(2)
    send(other_column[0], None, core_sem, (4, 0), to_core)
    for h in range(PIECES):
        column(3, h)
    for h in range(PIECES // 2, PIECES):
        send_on(1, other_column[0], h, mate_sem, (1, h), to_mate)
    to_other_core(3)
    crossed(1)
    crossed(2)
    plane(0)
    plane(1)
    crossed(3)
    plane(2)
    other_core(3, core_row)
    project(order[3] * 4 + 2 * x, 2)
    other_core(3, both_row)
    project(order[3] * 4 + 2 * (1 - x), 2)

    loads[4].wait()
    here = member(held[:, :, feat:feat + FLAGS].reshape(-1, FLAGS))
    for copy in summed:
        copy.wait_recv()
    projected = jnp.where(here > 0.5, part[...] + other[...], 0.0).T.astype(jnp.bfloat16)
    stores = []
    for lo in range(0, feat, WIDE):
        at = slice(lo, lo + WIDE)
        routed = held[:, :, at].reshape(-1, WIDE)
        comp = jnp.dot(projected, routed, preferred_element_type=jnp.float32)
        diag = jnp.sum(squares[:, at], axis=0, keepdims=True) / ROWS_E + damp_ref[:, at]
        updated = w_ref[:, at].astype(jnp.float32) + comp * (ETA / ROWS_E / diag)
        out_ref[:, at] = updated.astype(jnp.bfloat16) * keep[:, at]
        store = pltpu.make_async_copy(out_ref.at[:, at], out_hbm.at[0, :, at], store_sem.at[lo // WIDE])
        store.start()
        stores.append(store)

    finish(None)
    for copy in summed:
        copy.wait_send()

    @pl.when(inner == 1)
    def _():
        finish(1)

    @pl.when(inner == 0)
    def _():
        finish(0)

    for store in stores:
        store.wait()


def leave(from_hbm, to_hbm, slabs, in_sems, out_sems):
    count, rows = slabs.shape[0], slabs.shape[1]
    ins, outs = [], []
    for i in range(count):
        at = pl.ds(i * rows, rows)
        ins.append(pltpu.make_async_copy(from_hbm.at[0, at, :], slabs.at[i], in_sems.at[i]))
        outs.append(pltpu.make_async_copy(slabs.at[i], to_hbm.at[0, at, :], out_sems.at[i]))
        ins[i].start()
    for i in range(count):
        ins[i].wait()
        outs[i].start()
    for out in outs:
        out.wait()


def gathered(tokens, expert_ids, weight, mask_bits, damping):
    tok_count, feat = tokens.shape
    slab = weight.shape[1]
    blocks = 16
    total = blocks * tok_count
    dma = pltpu.SemaphoreType.DMA
    result = pl.pallas_call(
        kernel,
        out_shape=jax.ShapeDtypeStruct(weight.shape, jnp.bfloat16),
        in_specs=[pl.BlockSpec(memory_space=pltpu.HBM)] * 5,
        out_specs=pl.BlockSpec(memory_space=pl.ANY),
        scratch_shapes=[
            pltpu.VMEM((blocks, tok_count, feat + FLAGS), jnp.bfloat16),
            pltpu.VMEM((slab, feat), jnp.bfloat16),
            pltpu.VMEM((slab, feat), jnp.bfloat16),
            pltpu.VMEM((slab, feat), jnp.bfloat16),
            pltpu.VMEM((total, slab), jnp.float32),
            pltpu.VMEM((total, slab), jnp.float32),
            pltpu.VMEM((8, feat), jnp.float32),
            pltpu.VMEM((expert_ids.shape[1], tok_count), jnp.int32),
            pltpu.VMEM((expert_ids.shape[1], 128), jnp.int32),
            pltpu.VMEM((128, slab), jnp.int32),
            pltpu.VMEM((slab, 128), jnp.int32),
            pltpu.VMEM((1, feat), jnp.float32),
            pltpu.VMEM((slab, feat), jnp.bfloat16),
            dma((5,)),
            dma((blocks, PIECES)),
            dma((4, PIECES)),
            dma((8, PIECES)),
            dma((4, PIECES)),
            dma((2, PIECES)),
            dma((5,)),
            dma((5,)),
            dma((feat // WIDE,)),
        ],
        compiler_params=pltpu.CompilerParams(
            collective_id=0, has_side_effects=True, vmem_limit_bytes=62 * 1024 * 1024),
        cost_estimate=pl.CostEstimate(
            flops=4 * total * slab * feat, bytes_accessed=4 * slab * feat, transcendentals=0),
    )(tokens, expert_ids.T, weight, mask_bits.T, damping)
    return pl.pallas_call(
        leave,
        out_shape=jax.ShapeDtypeStruct(weight.shape, jnp.bfloat16),
        in_specs=[pl.BlockSpec(memory_space=pl.ANY)],
        out_specs=pl.BlockSpec(memory_space=pl.ANY),
        scratch_shapes=[pltpu.VMEM((8, slab // 8, feat), jnp.bfloat16), dma((8,)), dma((8,))],
        compiler_params=pltpu.CompilerParams(vmem_limit_bytes=62 * 1024 * 1024),
    )(result)


def solution(mesh):
    in_specs = (
        P(("expert", "hrow"), "hcol"),
        P(("expert", "hrow"), None),
        P(("expert", "hrow"), None, "hcol"),
        P(None, "hcol"),
        P(("expert", "hrow"), "hcol"),
    )
    out_specs = P(("expert", "hrow"), None, "hcol")
    line, cross = mesh.shape["expert"], mesh.shape["hrow"]

    def body(tokens, expert_ids, weight, mask_bits, damping):
        tok_count, top_count = expert_ids.shape
        capacity = 2 * tok_count * top_count // (line * cross * weight.shape[0])
        fits = line == 4 and cross == 4 and mesh.shape["hcol"] == 2 and weight.shape[0] == 1
        if fits and capacity >= tok_count:
            return gathered(tokens, expert_ids, weight, mask_bits, damping)
        return local(tokens, expert_ids, weight, mask_bits, damping)

    return jax.shard_map(body, mesh=mesh, in_specs=in_specs, out_specs=out_specs, check_vma=False)
```

```python
import functools

import jax
import jax.numpy as jnp
from jax import lax
from jax.experimental import pallas as pl
from jax.experimental.pallas import tpu as pltpu
from jax.sharding import PartitionSpec as P

ROWS_E = 128


ETA = 0.5


def unpack_bits(bits):
    bit_shifts = jnp.arange(32, dtype=jnp.int32)
    bit_flags = jnp.bitwise_and(jnp.right_shift(bits[:, :, None], bit_shifts[None, None, :]), 1)
    return bit_flags.reshape(bits.shape[0], bits.shape[1] * 32)


def route_rows(tokens, expert_ids, group_count, local_count):
    tok_count, top_count = expert_ids.shape
    expert_count = group_count * local_count
    capacity = 2 * tok_count * top_count // expert_count
    flat_ids = expert_ids.reshape(-1)
    one_hot = (flat_ids[:, None] == jnp.arange(expert_count, dtype=jnp.int32)[None, :]).astype(
        jnp.int32
    )
    prior_count = jnp.cumsum(one_hot, axis=0) - one_hot
    slot_index = jnp.sum(prior_count * one_hot, axis=1)
    group_of = flat_ids // local_count
    local_of = flat_ids % local_count
    target_slot = ((local_of * group_count + group_of) * capacity + slot_index).reshape(
        tok_count, top_count
    )
    slot_ids = jnp.arange(expert_count * capacity, dtype=jnp.int32)
    selector = jnp.any(slot_ids[:, None, None] == target_slot[None, :, :], axis=2).astype(
        jnp.bfloat16
    )
    packed = jnp.dot(selector, tokens, preferred_element_type=jnp.float32).astype(jnp.bfloat16)
    return packed.reshape(local_count, group_count, 1, capacity, tokens.shape[1])


def local(tokens, expert_ids, weight, mask_bits, damping):
    group_count = lax.axis_size(("expert", "hrow"))
    local_experts = weight.shape[0]
    feat_width = tokens.shape[1]
    slab_rows = weight.shape[1]
    packed = route_rows(tokens, expert_ids, group_count, local_experts)
    keep_flags = unpack_bits(mask_bits)
    keep_mask = keep_flags[None, :, :] == 1
    pruned = jnp.where(keep_mask, jnp.zeros_like(weight), weight)
    block = lax.all_to_all(packed, ("expert", "hrow"), split_axis=1, concat_axis=2, tiled=True)
    partials = jnp.einsum("esf,exgcf->exgcs", pruned, block, preferred_element_type=jnp.float32)
    slot_count = block.shape[1] * block.shape[2] * block.shape[3]
    routed = block.reshape(local_experts, slot_count, feat_width)
    partials = partials.reshape(local_experts, slot_count, slab_rows)
    projected = lax.psum(partials, "hcol").astype(jnp.bfloat16)
    comp_term = (
        jnp.einsum("ers,erf->esf", projected, routed, preferred_element_type=jnp.float32) / ROWS_E
    )
    diag_scale = (
        jnp.einsum("erf,erf->ef", routed, routed, preferred_element_type=jnp.float32) / ROWS_E
        + damping
    )
    updated = weight.astype(jnp.float32) + ETA * comp_term / diag_scale[:, None, :]
    return jnp.where(keep_mask, updated, jnp.float32(0.0)).astype(jnp.bfloat16)


MESH = pl.DeviceIdType.MESH
FLAGS = 128
CHUNK = 256
WIDE = 512
PIECES = 4


def kernel(tok_hbm, ids_hbm, w_hbm, bits_hbm, damp_hbm, out_hbm,
           held, w_ref, pruned, keep, part, other, squares, ids_ref, wide_ids, bits_ref, words, damp_ref, out_ref,
           load_sem, recv_sem, x_sem, core_sem, mate_sem, across_sem, y_send, y_recv, store_sem):
    z, cross, y = lax.axis_index("expert"), lax.axis_index("hrow"), lax.axis_index("hcol")
    tok_count, feat = tok_hbm.shape
    slab = w_hbm.shape[1]
    quarter = feat // (128 * PIECES) * 128
    spans = [(i * quarter, quarter) for i in range(PIECES - 1)]
    spans.append(((PIECES - 1) * quarter, feat + FLAGS - (PIECES - 1) * quarter))
    whole = (0, feat + FLAGS)
    x, core = cross // 2, cross % 2
    upper = z // 2
    inner = (z + 1) // 2 % 2
    mate = 4 * upper + 1 - z
    across = 3 - z
    order = (z, mate, 2 - upper, 3 - 3 * upper)
    x_row, core_row = (1 - x) * 2 + core, x * 2 + 1 - core
    both_row = (1 - x) * 2 + 1 - core
    to_mate, to_across = (mate, cross, y), (across, cross, y)
    to_x, to_core, to_y = (z, x_row, y), (z, core_row, y), (z, cross, 1 - y)
    mine = z * 4 + cross

    loads = [
        pltpu.make_async_copy(tok_hbm, held.at[mine, :, pl.ds(0, feat)], load_sem.at[0]),
        pltpu.make_async_copy(ids_hbm, ids_ref, load_sem.at[1]),
        pltpu.make_async_copy(bits_hbm, bits_ref.at[pl.ds(0, bits_hbm.shape[0]), :], load_sem.at[2]),
        pltpu.make_async_copy(w_hbm.at[0], w_ref, load_sem.at[3]),
        pltpu.make_async_copy(damp_hbm, damp_ref, load_sem.at[4]),
    ]
    barrier = pltpu.get_barrier_semaphore()
    for device in (to_mate, to_x, to_core, to_y):
        pl.semaphore_signal(barrier, inc=1, device_id=device, device_id_type=MESH)

    @pl.when(inner == 1)
    def _():
        pl.semaphore_signal(barrier, inc=1, device_id=to_across, device_id_type=MESH)

    for load in loads:
        load.start()

    def block(number, h, sem, device):
        lo, size = whole if h is None else spans[h]
        piece = held.at[number, :, pl.ds(lo, size)]
        return pltpu.make_async_remote_copy(
            src_ref=piece, dst_ref=piece, send_sem=sem, recv_sem=recv_sem.at[number, h or 0],
            device_id=device, device_id_type=MESH)

    def arrived(number, h):
        block(number, h, x_sem.at[0, 0], to_x).wait_recv()

    sent = {None: [], 0: [], 1: []}
    own_column = [order[step] * 4 + cross for step in range(4)]
    other_column = [order[step] * 4 + x_row for step in range(4)]

    def send(number, h, sem, at, device, where=None):
        block(number, h, sem.at[at], device).start()
        sent[where].append((number, h, sem, at, device))

    def send_on(kind, number, h, sem, at, device):
        @pl.when(inner == kind)
        def _():
            send(number, h, sem, at, device, kind)

    def finish(where):
        for number, h, sem, at, device in sent[where]:
            block(number, h, sem.at[at], device).wait_send()

    def spread(h):
        send_on(1, mine, h, across_sem, (0, h), to_across)
        if h < PIECES // 2:
            send(mine, h, mate_sem, (0, h), to_mate)
        else:
            send_on(0, mine, h, mate_sem, (0, h), to_mate)
        send(mine, h, x_sem, (0, h), to_x)

    def column(step, h, where=None):
        number = own_column[step]
        arrived(number, h)
        if where != 0:
            sem, device = (across_sem, to_across) if step == 1 else (mate_sem, to_mate)
            at = (1, h) if step == 1 else (step, h)
            if where == 1:
                send(number, h, sem, at, device, 1)
            else:
                send_on(1, number, h, sem, at, device)
        if step > 1 or (where == 0 and h < PIECES // 2):
            send(number, h, x_sem, (step, h), to_x, where)

    def to_other_core(step):
        send(own_column[step], None, core_sem, (step, 0), to_core)

    def crossed(step):
        for h in range(PIECES):
            arrived(other_column[step], h)
            if step == 3:
                send(other_column[step], h, core_sem, (4 + step, h), to_core)
        if step < 3:
            send(other_column[step], None, core_sem, (4 + step, 0), to_core)

    def rows_of(first, count):
        return pl.ds(pl.multiple_of(first * tok_count, tok_count), count * tok_count)

    def y_copy(first, count, which):
        rows = rows_of(first, count)
        return pltpu.make_async_remote_copy(
            src_ref=part.at[rows, :], dst_ref=other.at[rows, :], send_sem=y_send.at[which],
            recv_sem=y_recv.at[which], device_id=to_y, device_id_type=MESH)

    def member(flags):
        lane = lax.broadcasted_iota(jnp.int32, flags.shape, 1)
        return jnp.sum(jnp.where(lane == mine, flags.astype(jnp.float32), 0.0), axis=1, keepdims=True)

    summed = []

    def project(first, count):
        rows, blocks = count * tok_count, pl.ds(first, count)
        tokens = held[blocks, :, 0:feat].reshape(rows, feat)
        part[rows_of(first, count), :] = lax.dot_general(
            pruned[...], tokens, (((1,), (1,)), ((), ())), preferred_element_type=jnp.float32).T
        copy = y_copy(first, count, len(summed))
        copy.start()
        summed.append(copy)
        here = member(held[blocks, :, feat:feat + FLAGS].reshape(rows, FLAGS))
        for lo in range(0, feat, CHUNK):
            piece = held[blocks, :, lo:lo + CHUNK].reshape(rows, CHUNK).astype(jnp.float32)
            total = jnp.sum((piece * piece * here).reshape(-1, 8, CHUNK), axis=0)
            squares[:, lo:lo + CHUNK] = total if len(summed) == 1 else squares[:, lo:lo + CHUNK] + total

    def other_core(step, row):
        for h in range(PIECES) if step == 3 and row is both_row else (None,):
            arrived(order[step] * 4 + row, h)

    def plane(step):
        other_core(step, core_row)
        other_core(step, both_row)
        project(order[step] * 4, 4)

    loads[1].wait()
    wide_ids[...] = jnp.full_like(wide_ids, -1)
    wide_ids[:, 0:tok_count] = ids_ref[...]
    expert = lax.broadcasted_iota(jnp.int32, (FLAGS, 128), 0)
    named = jnp.zeros((FLAGS, 128), jnp.float32)
    for k in range(ids_ref.shape[0]):
        named = jnp.where(wide_ids[k:k + 1, :] == expert, 1.0, named)
    held[mine, :, feat:feat + FLAGS] = named.T[0:tok_count, :].astype(jnp.bfloat16)
    loads[0].wait()
    pl.semaphore_wait(barrier, 4 + inner)

    for h in range(PIECES):
        spread(h)
    to_other_core(0)

    filled = bits_hbm.shape[0]
    if filled < 128:
        bits_ref[filled:128, :] = jnp.zeros((128 - filled, slab), jnp.int32)
    loads[2].wait()
    loads[3].wait()
    words[...] = bits_ref[...].T

    spot = lax.broadcasted_iota(jnp.int32, (1, 128), 1)
    group = jnp.right_shift(spot, 5)
    probe = jnp.left_shift(jnp.int32(1), jnp.bitwise_and(spot, 31))

    def unpack(j, carry):
        at = pl.ds(pl.multiple_of(j * 128, 128), 128)
        index = jnp.broadcast_to(group + 4 * j, (slab, 128))
        word = jnp.take_along_axis(words[...], index, axis=1)
        flag = jnp.where(jnp.bitwise_and(word, probe) != 0, 1.0, 0.0).astype(jnp.bfloat16)
        keep[:, at] = flag
        pruned[:, at] = w_ref[:, at] * (jnp.bfloat16(1.0) - flag)
        return carry

    steps = feat // 128
    lax.fori_loop(0, steps, unpack, 0)
    @pl.when(inner == 1)
    def _():
        for h in range(PIECES):
            column(1, h, 1)
            column(2, h, 1)
        for h in range(PIECES):
            arrived(other_column[0], h)

    @pl.when(inner == 0)
    def _():
        for h in range(PIECES):
            if h < PIECES // 2:
                column(1, h, 0)
            arrived(other_column[0], h)
            send(other_column[0], h, mate_sem, (1, h), to_mate, 0)
        for h in range(PIECES):
            column(2, h, 0)

    to_other_core(2)
    send(other_column[0], None, core_sem, (4, 0), to_core)
    for h in range(PIECES):
        column(3, h)
    for h in range(PIECES // 2, PIECES):
        send_on(1, mine, h, mate_sem, (0, h), to_mate)
    for h in range(PIECES // 2, PIECES):
        send_on(1, other_column[0], h, mate_sem, (1, h), to_mate)
    to_other_core(3)
    crossed(2)
    plane(0)

    @pl.when(inner == 0)
    def _():
        for h in range(PIECES // 2, PIECES):
            arrived(own_column[1], h)

    to_other_core(1)
    crossed(3)
    plane(2)
    crossed(1)
    for step in (3, 1):
        other_core(step, core_row)
        project(order[step] * 4 + 2 * x, 2)
    for step in (3, 1):
        other_core(step, both_row)
        project(order[step] * 4 + 2 * (1 - x), 2)

    loads[4].wait()
    here = member(held[:, :, feat:feat + FLAGS].reshape(-1, FLAGS))
    for copy in summed:
        copy.wait_recv()
    projected = jnp.where(here > 0.5, part[...] + other[...], 0.0).T.astype(jnp.bfloat16)
    stores = []
    for lo in range(0, feat, WIDE):
        at = slice(lo, lo + WIDE)
        routed = held[:, :, at].reshape(-1, WIDE)
        comp = jnp.dot(projected, routed, preferred_element_type=jnp.float32)
        diag = jnp.sum(squares[:, at], axis=0, keepdims=True) / ROWS_E + damp_ref[:, at]
        updated = w_ref[:, at].astype(jnp.float32) + comp * (ETA / ROWS_E / diag)
        out_ref[:, at] = updated.astype(jnp.bfloat16) * keep[:, at]
        store = pltpu.make_async_copy(out_ref.at[:, at], out_hbm.at[0, :, at], store_sem.at[lo // WIDE])
        store.start()
        stores.append(store)

    finish(None)
    for copy in summed:
        copy.wait_send()

    @pl.when(inner == 1)
    def _():
        finish(1)

    @pl.when(inner == 0)
    def _():
        finish(0)

    for store in stores:
        store.wait()


def leave(from_hbm, to_hbm, slabs, in_sems, out_sems):
    count, rows = slabs.shape[0], slabs.shape[1]
    ins, outs = [], []
    for i in range(count):
        at = pl.ds(i * rows, rows)
        ins.append(pltpu.make_async_copy(from_hbm.at[0, at, :], slabs.at[i], in_sems.at[i]))
        outs.append(pltpu.make_async_copy(slabs.at[i], to_hbm.at[0, at, :], out_sems.at[i]))
        ins[i].start()
    for i in range(count):
        ins[i].wait()
        outs[i].start()
    for out in outs:
        out.wait()


def gathered(tokens, expert_ids, weight, mask_bits, damping):
    tok_count, feat = tokens.shape
    slab = weight.shape[1]
    blocks = 16
    total = blocks * tok_count
    dma = pltpu.SemaphoreType.DMA
    result = pl.pallas_call(
        kernel,
        out_shape=jax.ShapeDtypeStruct(weight.shape, jnp.bfloat16),
        in_specs=[pl.BlockSpec(memory_space=pltpu.HBM)] * 5,
        out_specs=pl.BlockSpec(memory_space=pl.ANY),
        scratch_shapes=[
            pltpu.VMEM((blocks, tok_count, feat + FLAGS), jnp.bfloat16),
            pltpu.VMEM((slab, feat), jnp.bfloat16),
            pltpu.VMEM((slab, feat), jnp.bfloat16),
            pltpu.VMEM((slab, feat), jnp.bfloat16),
            pltpu.VMEM((total, slab), jnp.float32),
            pltpu.VMEM((total, slab), jnp.float32),
            pltpu.VMEM((8, feat), jnp.float32),
            pltpu.VMEM((expert_ids.shape[1], tok_count), jnp.int32),
            pltpu.VMEM((expert_ids.shape[1], 128), jnp.int32),
            pltpu.VMEM((128, slab), jnp.int32),
            pltpu.VMEM((slab, 128), jnp.int32),
            pltpu.VMEM((1, feat), jnp.float32),
            pltpu.VMEM((slab, feat), jnp.bfloat16),
            dma((5,)),
            dma((blocks, PIECES)),
            dma((4, PIECES)),
            dma((8, PIECES)),
            dma((4, PIECES)),
            dma((2, PIECES)),
            dma((6,)),
            dma((6,)),
            dma((feat // WIDE,)),
        ],
        compiler_params=pltpu.CompilerParams(
            collective_id=0, has_side_effects=True, vmem_limit_bytes=62 * 1024 * 1024),
        cost_estimate=pl.CostEstimate(
            flops=4 * total * slab * feat, bytes_accessed=4 * slab * feat, transcendentals=0),
    )(tokens, expert_ids.T, weight, mask_bits.T, damping)
    return pl.pallas_call(
        leave,
        out_shape=jax.ShapeDtypeStruct(weight.shape, jnp.bfloat16),
        in_specs=[pl.BlockSpec(memory_space=pl.ANY)],
        out_specs=pl.BlockSpec(memory_space=pl.ANY),
        scratch_shapes=[pltpu.VMEM((8, slab // 8, feat), jnp.bfloat16), dma((8,)), dma((8,))],
        compiler_params=pltpu.CompilerParams(vmem_limit_bytes=62 * 1024 * 1024),
    )(result)


def solution(mesh):
    in_specs = (
        P(("expert", "hrow"), "hcol"),
        P(("expert", "hrow"), None),
        P(("expert", "hrow"), None, "hcol"),
        P(None, "hcol"),
        P(("expert", "hrow"), "hcol"),
    )
    out_specs = P(("expert", "hrow"), None, "hcol")
    line, cross = mesh.shape["expert"], mesh.shape["hrow"]

    def body(tokens, expert_ids, weight, mask_bits, damping):
        tok_count, top_count = expert_ids.shape
        capacity = 2 * tok_count * top_count // (line * cross * weight.shape[0])
        fits = line == 4 and cross == 4 and mesh.shape["hcol"] == 2 and weight.shape[0] == 1
        if fits and capacity >= tok_count:
            return gathered(tokens, expert_ids, weight, mask_bits, damping)
        return local(tokens, expert_ids, weight, mask_bits, damping)

    return jax.shard_map(body, mesh=mesh, in_specs=in_specs, out_specs=out_specs, check_vma=False)
```

```python
import functools

import jax
import jax.numpy as jnp
from jax import lax
from jax.experimental import pallas as pl
from jax.experimental.pallas import tpu as pltpu
from jax.sharding import PartitionSpec as P

ROWS_E = 128


ETA = 0.5


def unpack_bits(bits):
    bit_shifts = jnp.arange(32, dtype=jnp.int32)
    bit_flags = jnp.bitwise_and(jnp.right_shift(bits[:, :, None], bit_shifts[None, None, :]), 1)
    return bit_flags.reshape(bits.shape[0], bits.shape[1] * 32)


def route_rows(tokens, expert_ids, group_count, local_count):
    tok_count, top_count = expert_ids.shape
    expert_count = group_count * local_count
    capacity = 2 * tok_count * top_count // expert_count
    flat_ids = expert_ids.reshape(-1)
    one_hot = (flat_ids[:, None] == jnp.arange(expert_count, dtype=jnp.int32)[None, :]).astype(
        jnp.int32
    )
    prior_count = jnp.cumsum(one_hot, axis=0) - one_hot
    slot_index = jnp.sum(prior_count * one_hot, axis=1)
    group_of = flat_ids // local_count
    local_of = flat_ids % local_count
    target_slot = ((local_of * group_count + group_of) * capacity + slot_index).reshape(
        tok_count, top_count
    )
    slot_ids = jnp.arange(expert_count * capacity, dtype=jnp.int32)
    selector = jnp.any(slot_ids[:, None, None] == target_slot[None, :, :], axis=2).astype(
        jnp.bfloat16
    )
    packed = jnp.dot(selector, tokens, preferred_element_type=jnp.float32).astype(jnp.bfloat16)
    return packed.reshape(local_count, group_count, 1, capacity, tokens.shape[1])


def local(tokens, expert_ids, weight, mask_bits, damping):
    group_count = lax.axis_size(("expert", "hrow"))
    local_experts = weight.shape[0]
    feat_width = tokens.shape[1]
    slab_rows = weight.shape[1]
    packed = route_rows(tokens, expert_ids, group_count, local_experts)
    keep_flags = unpack_bits(mask_bits)
    keep_mask = keep_flags[None, :, :] == 1
    pruned = jnp.where(keep_mask, jnp.zeros_like(weight), weight)
    block = lax.all_to_all(packed, ("expert", "hrow"), split_axis=1, concat_axis=2, tiled=True)
    partials = jnp.einsum("esf,exgcf->exgcs", pruned, block, preferred_element_type=jnp.float32)
    slot_count = block.shape[1] * block.shape[2] * block.shape[3]
    routed = block.reshape(local_experts, slot_count, feat_width)
    partials = partials.reshape(local_experts, slot_count, slab_rows)
    projected = lax.psum(partials, "hcol").astype(jnp.bfloat16)
    comp_term = (
        jnp.einsum("ers,erf->esf", projected, routed, preferred_element_type=jnp.float32) / ROWS_E
    )
    diag_scale = (
        jnp.einsum("erf,erf->ef", routed, routed, preferred_element_type=jnp.float32) / ROWS_E
        + damping
    )
    updated = weight.astype(jnp.float32) + ETA * comp_term / diag_scale[:, None, :]
    return jnp.where(keep_mask, updated, jnp.float32(0.0)).astype(jnp.bfloat16)


MESH = pl.DeviceIdType.MESH
FLAGS = 128
CHUNK = 256
WIDE = 512
PIECES = 4


def kernel(tok_hbm, ids_hbm, w_hbm, bits_hbm, damp_hbm, proj_hbm, scale_hbm, keep_hbm, rows_hbm,
           held, w_ref, pruned, keep, part, other, squares, ids_ref, wide_ids, bits_ref, words, damp_ref, proj_ref, scale_ref,
           load_sem, recv_sem, x_sem, core_sem, mate_sem, across_sem, y_send, y_recv, store_sem):
    z, cross, y = lax.axis_index("expert"), lax.axis_index("hrow"), lax.axis_index("hcol")
    tok_count, feat = tok_hbm.shape
    slab = w_hbm.shape[1]
    quarter = feat // (128 * PIECES) * 128
    spans = [(i * quarter, quarter) for i in range(PIECES - 1)]
    spans.append(((PIECES - 1) * quarter, feat + FLAGS - (PIECES - 1) * quarter))
    whole = (0, feat + FLAGS)
    x, core = cross // 2, cross % 2
    upper = z // 2
    inner = (z + 1) // 2 % 2
    mate = 4 * upper + 1 - z
    across = 3 - z
    order = (z, mate, 2 - upper, 3 - 3 * upper)
    x_row, core_row = (1 - x) * 2 + core, x * 2 + 1 - core
    both_row = (1 - x) * 2 + 1 - core
    to_mate, to_across = (mate, cross, y), (across, cross, y)
    to_x, to_core, to_y = (z, x_row, y), (z, core_row, y), (z, cross, 1 - y)
    mine = z * 4 + cross

    loads = [
        pltpu.make_async_copy(tok_hbm, held.at[mine, :, pl.ds(0, feat)], load_sem.at[0]),
        pltpu.make_async_copy(ids_hbm, ids_ref, load_sem.at[1]),
        pltpu.make_async_copy(bits_hbm, bits_ref.at[pl.ds(0, bits_hbm.shape[0]), :], load_sem.at[2]),
        pltpu.make_async_copy(w_hbm.at[0], w_ref, load_sem.at[3]),
        pltpu.make_async_copy(damp_hbm, damp_ref, load_sem.at[4]),
    ]
    barrier = pltpu.get_barrier_semaphore()
    for device in (to_mate, to_x, to_core, to_y):
        pl.semaphore_signal(barrier, inc=1, device_id=device, device_id_type=MESH)

    @pl.when(inner == 1)
    def _():
        pl.semaphore_signal(barrier, inc=1, device_id=to_across, device_id_type=MESH)

    for load in loads:
        load.start()

    def block(number, h, sem, device):
        lo, size = whole if h is None else spans[h]
        piece = held.at[number, :, pl.ds(lo, size)]
        return pltpu.make_async_remote_copy(
            src_ref=piece, dst_ref=piece, send_sem=sem, recv_sem=recv_sem.at[number, h or 0],
            device_id=device, device_id_type=MESH)

    def arrived(number, h):
        block(number, h, x_sem.at[0, 0], to_x).wait_recv()

    sent = {None: [], 0: [], 1: []}
    own_column = [order[step] * 4 + cross for step in range(4)]
    other_column = [order[step] * 4 + x_row for step in range(4)]

    def send(number, h, sem, at, device, where=None):
        block(number, h, sem.at[at], device).start()
        sent[where].append((number, h, sem, at, device))

    def send_on(kind, number, h, sem, at, device):
        @pl.when(inner == kind)
        def _():
            send(number, h, sem, at, device, kind)

    def finish(where):
        for number, h, sem, at, device in sent[where]:
            block(number, h, sem.at[at], device).wait_send()

    def spread(h):
        send_on(1, mine, h, across_sem, (0, h), to_across)
        send(mine, h, mate_sem, (0, h), to_mate)
        send(mine, h, x_sem, (0, h), to_x)

    def column(step, h, where=None):
        number = own_column[step]
        arrived(number, h)
        if where != 0:
            sem, device = (across_sem, to_across) if step == 1 else (mate_sem, to_mate)
            at = (1, h) if step == 1 else (step, h)
            if where == 1:
                send(number, h, sem, at, device, 1)
            else:
                send_on(1, number, h, sem, at, device)
        if step > 1 or (where == 0 and h < PIECES // 2):
            send(number, h, x_sem, (step, h), to_x, where)

    def to_other_core(step):
        send(own_column[step], None, core_sem, (step, 0), to_core)

    def crossed(step):
        for h in range(PIECES):
            arrived(other_column[step], h)
            if step == 3:
                send(other_column[step], h, core_sem, (4 + step, h), to_core)
        if step < 3:
            send(other_column[step], None, core_sem, (4 + step, 0), to_core)

    def rows_of(first, count):
        return pl.ds(pl.multiple_of(first * tok_count, tok_count), count * tok_count)

    def y_copy(first, count, which):
        rows = rows_of(first, count)
        return pltpu.make_async_remote_copy(
            src_ref=part.at[rows, :], dst_ref=other.at[rows, :], send_sem=y_send.at[which],
            recv_sem=y_recv.at[which], device_id=to_y, device_id_type=MESH)

    def member(flags):
        lane = lax.broadcasted_iota(jnp.int32, flags.shape, 1)
        return jnp.sum(jnp.where(lane == mine, flags.astype(jnp.float32), 0.0), axis=1, keepdims=True)

    summed, stores = [], []

    def store(src, dst):
        copy = pltpu.make_async_copy(src, dst, store_sem.at[len(stores)])
        copy.start()
        stores.append(copy)

    def project(first, count):
        rows, blocks = count * tok_count, pl.ds(first, count)
        tokens = held[blocks, :, 0:feat].reshape(rows, feat)
        part[rows_of(first, count), :] = lax.dot_general(
            pruned[...], tokens, (((1,), (1,)), ((), ())), preferred_element_type=jnp.float32).T
        copy = y_copy(first, count, len(summed))
        copy.start()
        summed.append(copy)
        store(held.at[blocks, :, pl.ds(0, feat)], rows_hbm.at[blocks])
        here = member(held[blocks, :, feat:feat + FLAGS].reshape(rows, FLAGS))
        for lo in range(0, feat, CHUNK):
            piece = held[blocks, :, lo:lo + CHUNK].reshape(rows, CHUNK).astype(jnp.float32)
            total = jnp.sum((piece * piece * here).reshape(-1, 8, CHUNK), axis=0)
            squares[:, lo:lo + CHUNK] = total if len(summed) == 1 else squares[:, lo:lo + CHUNK] + total

    def other_core(step, row):
        for h in range(PIECES) if step == 3 and row is both_row else (None,):
            arrived(order[step] * 4 + row, h)

    def plane(step):
        other_core(step, core_row)
        other_core(step, both_row)
        project(order[step] * 4, 4)

    loads[1].wait()
    wide_ids[...] = jnp.full_like(wide_ids, -1)
    wide_ids[:, 0:tok_count] = ids_ref[...]
    expert = lax.broadcasted_iota(jnp.int32, (FLAGS, 128), 0)
    named = jnp.zeros((FLAGS, 128), jnp.float32)
    for k in range(ids_ref.shape[0]):
        named = jnp.where(wide_ids[k:k + 1, :] == expert, 1.0, named)
    held[mine, :, feat:feat + FLAGS] = named.T[0:tok_count, :].astype(jnp.bfloat16)
    loads[0].wait()
    pl.semaphore_wait(barrier, 4 + inner)

    for h in range(PIECES):
        spread(h)
    to_other_core(0)

    filled = bits_hbm.shape[0]
    if filled < 128:
        bits_ref[filled:128, :] = jnp.zeros((128 - filled, slab), jnp.int32)
    loads[2].wait()
    loads[3].wait()
    words[...] = bits_ref[...].T

    spot = lax.broadcasted_iota(jnp.int32, (1, 128), 1)
    group = jnp.right_shift(spot, 5)
    probe = jnp.left_shift(jnp.int32(1), jnp.bitwise_and(spot, 31))

    def unpack(j, carry):
        at = pl.ds(pl.multiple_of(j * 128, 128), 128)
        index = jnp.broadcast_to(group + 4 * j, (slab, 128))
        word = jnp.take_along_axis(words[...], index, axis=1)
        flag = jnp.where(jnp.bitwise_and(word, probe) != 0, 1.0, 0.0).astype(jnp.bfloat16)
        keep[:, at] = flag
        pruned[:, at] = w_ref[:, at] * (jnp.bfloat16(1.0) - flag)
        return carry

    steps = feat // 128
    lax.fori_loop(0, steps, unpack, 0)
    store(keep, keep_hbm)
    @pl.when(inner == 1)
    def _():
        for h in range(PIECES):
            column(1, h, 1)
            column(2, h, 1)
        for h in range(PIECES):
            arrived(other_column[0], h)

    @pl.when(inner == 0)
    def _():
        for h in range(PIECES):
            column(1, h, 0)
            arrived(other_column[0], h)
            send(other_column[0], h, mate_sem, (1, h), to_mate, 0)
        for h in range(PIECES):
            column(2, h, 0)

    to_other_core(1)
    to_other_core(2)
    send(other_column[0], None, core_sem, (4, 0), to_core)
    for h in range(PIECES):
        column(3, h)
    for h in range(PIECES // 2, PIECES):
        send_on(1, other_column[0], h, mate_sem, (1, h), to_mate)
    to_other_core(3)
    crossed(1)
    crossed(2)
    plane(0)
    plane(1)
    crossed(3)
    plane(2)
    other_core(3, core_row)
    project(order[3] * 4 + 2 * x, 2)
    other_core(3, both_row)
    project(order[3] * 4 + 2 * (1 - x), 2)

    loads[4].wait()
    diag = jnp.sum(squares[...], axis=0, keepdims=True) / ROWS_E + damp_ref[...]
    scale_ref[...] = ETA / ROWS_E / diag
    store(scale_ref, scale_hbm)
    here = member(held[:, :, feat:feat + FLAGS].reshape(-1, FLAGS))
    for copy in summed:
        copy.wait_recv()
    projected = jnp.where(here > 0.5, part[...] + other[...], 0.0).T.astype(jnp.bfloat16)
    proj_ref[...] = projected
    store(proj_ref, proj_hbm)
    finish(None)
    for copy in summed:
        copy.wait_send()

    @pl.when(inner == 1)
    def _():
        finish(1)

    @pl.when(inner == 0)
    def _():
        finish(0)

    for copy in stores:
        copy.wait()


def compensate(proj_hbm, scale_hbm, keep_hbm, rows_hbm, w_hbm, out_hbm,
               proj_ref, scale_ref, keep, rows, w_ref, out_ref, head_sem, load_sem, store_sem):
    feat = rows_hbm.shape[1]
    heads = [
        pltpu.make_async_copy(proj_hbm, proj_ref, head_sem.at[0]),
        pltpu.make_async_copy(scale_hbm, scale_ref, head_sem.at[1]),
    ]
    for copy in heads:
        copy.start()
    loads, stores = [], []
    for i in range(feat // WIDE):
        at = slice(i * WIDE, (i + 1) * WIDE)
        loads.append([
            pltpu.make_async_copy(rows_hbm.at[:, at], rows.at[:, at], load_sem.at[i, 0]),
            pltpu.make_async_copy(w_hbm.at[0, :, at], w_ref.at[:, at], load_sem.at[i, 1]),
            pltpu.make_async_copy(keep_hbm.at[:, at], keep.at[:, at], load_sem.at[i, 2]),
        ])
        for copy in loads[i]:
            copy.start()
    for copy in heads:
        copy.wait()
    for i in range(feat // WIDE):
        at = slice(i * WIDE, (i + 1) * WIDE)
        for copy in loads[i]:
            copy.wait()
        comp = jnp.dot(proj_ref[...], rows[:, at], preferred_element_type=jnp.float32)
        updated = w_ref[:, at].astype(jnp.float32) + comp * scale_ref[:, at]
        out_ref[:, at] = updated.astype(jnp.bfloat16) * keep[:, at]
        copy = pltpu.make_async_copy(out_ref.at[:, at], out_hbm.at[0, :, at], store_sem.at[i])
        copy.start()
        stores.append(copy)
    for copy in stores:
        copy.wait()


def gathered(tokens, expert_ids, weight, mask_bits, damping):
    tok_count, feat = tokens.shape
    slab = weight.shape[1]
    blocks = 16
    total = blocks * tok_count
    dma = pltpu.SemaphoreType.DMA
    projected, scale, keep, rows = pl.pallas_call(
        kernel,
        out_shape=[
            jax.ShapeDtypeStruct((slab, total), jnp.bfloat16),
            jax.ShapeDtypeStruct((1, feat), jnp.float32),
            jax.ShapeDtypeStruct((slab, feat), jnp.bfloat16),
            jax.ShapeDtypeStruct((blocks, tok_count, feat), jnp.bfloat16),
        ],
        in_specs=[pl.BlockSpec(memory_space=pltpu.HBM)] * 5,
        out_specs=[pl.BlockSpec(memory_space=pl.ANY)] * 4,
        scratch_shapes=[
            pltpu.VMEM((blocks, tok_count, feat + FLAGS), jnp.bfloat16),
            pltpu.VMEM((slab, feat), jnp.bfloat16),
            pltpu.VMEM((slab, feat), jnp.bfloat16),
            pltpu.VMEM((slab, feat), jnp.bfloat16),
            pltpu.VMEM((total, slab), jnp.float32),
            pltpu.VMEM((total, slab), jnp.float32),
            pltpu.VMEM((8, feat), jnp.float32),
            pltpu.VMEM((expert_ids.shape[1], tok_count), jnp.int32),
            pltpu.VMEM((expert_ids.shape[1], 128), jnp.int32),
            pltpu.VMEM((128, slab), jnp.int32),
            pltpu.VMEM((slab, 128), jnp.int32),
            pltpu.VMEM((1, feat), jnp.float32),
            pltpu.VMEM((slab, total), jnp.bfloat16),
            pltpu.VMEM((1, feat), jnp.float32),
            dma((5,)),
            dma((blocks, PIECES)),
            dma((4, PIECES)),
            dma((8, PIECES)),
            dma((4, PIECES)),
            dma((2, PIECES)),
            dma((5,)),
            dma((5,)),
            dma((8,)),
        ],
        compiler_params=pltpu.CompilerParams(
            collective_id=0, has_side_effects=True, vmem_limit_bytes=62 * 1024 * 1024),
        cost_estimate=pl.CostEstimate(
            flops=4 * total * slab * feat, bytes_accessed=4 * slab * feat, transcendentals=0),
    )(tokens, expert_ids.T, weight, mask_bits.T, damping)
    spare = pltpu.VMEM((slab, feat), jnp.bfloat16)
    return pl.pallas_call(
        compensate,
        out_shape=jax.ShapeDtypeStruct(weight.shape, jnp.bfloat16),
        in_specs=[pl.BlockSpec(memory_space=pltpu.HBM)] * 5,
        out_specs=pl.BlockSpec(memory_space=pl.ANY),
        scratch_shapes=[
            pltpu.VMEM((slab, total), jnp.bfloat16), pltpu.VMEM((1, feat), jnp.float32), spare,
            pltpu.VMEM((total, feat), jnp.bfloat16), spare, spare,
            dma((2,)), dma((feat // WIDE, 3)), dma((feat // WIDE,)),
        ],
        compiler_params=pltpu.CompilerParams(vmem_limit_bytes=62 * 1024 * 1024),
    )(projected, scale, keep, rows.reshape(total, feat), weight)


def solution(mesh):
    in_specs = (
        P(("expert", "hrow"), "hcol"),
        P(("expert", "hrow"), None),
        P(("expert", "hrow"), None, "hcol"),
        P(None, "hcol"),
        P(("expert", "hrow"), "hcol"),
    )
    out_specs = P(("expert", "hrow"), None, "hcol")
    line, cross = mesh.shape["expert"], mesh.shape["hrow"]

    def body(tokens, expert_ids, weight, mask_bits, damping):
        tok_count, top_count = expert_ids.shape
        capacity = 2 * tok_count * top_count // (line * cross * weight.shape[0])
        fits = line == 4 and cross == 4 and mesh.shape["hcol"] == 2 and weight.shape[0] == 1
        if fits and capacity >= tok_count:
            return gathered(tokens, expert_ids, weight, mask_bits, damping)
        return local(tokens, expert_ids, weight, mask_bits, damping)

    return jax.shard_map(body, mesh=mesh, in_specs=in_specs, out_specs=out_specs, check_vma=False)
```

```python
import functools

import jax
import jax.numpy as jnp
from jax import lax
from jax.experimental import pallas as pl
from jax.experimental.pallas import tpu as pltpu
from jax.sharding import PartitionSpec as P

ROWS_E = 128


ETA = 0.5


def unpack_bits(bits):
    bit_shifts = jnp.arange(32, dtype=jnp.int32)
    bit_flags = jnp.bitwise_and(jnp.right_shift(bits[:, :, None], bit_shifts[None, None, :]), 1)
    return bit_flags.reshape(bits.shape[0], bits.shape[1] * 32)


def route_rows(tokens, expert_ids, group_count, local_count):
    tok_count, top_count = expert_ids.shape
    expert_count = group_count * local_count
    capacity = 2 * tok_count * top_count // expert_count
    flat_ids = expert_ids.reshape(-1)
    one_hot = (flat_ids[:, None] == jnp.arange(expert_count, dtype=jnp.int32)[None, :]).astype(
        jnp.int32
    )
    prior_count = jnp.cumsum(one_hot, axis=0) - one_hot
    slot_index = jnp.sum(prior_count * one_hot, axis=1)
    group_of = flat_ids // local_count
    local_of = flat_ids % local_count
    target_slot = ((local_of * group_count + group_of) * capacity + slot_index).reshape(
        tok_count, top_count
    )
    slot_ids = jnp.arange(expert_count * capacity, dtype=jnp.int32)
    selector = jnp.any(slot_ids[:, None, None] == target_slot[None, :, :], axis=2).astype(
        jnp.bfloat16
    )
    packed = jnp.dot(selector, tokens, preferred_element_type=jnp.float32).astype(jnp.bfloat16)
    return packed.reshape(local_count, group_count, 1, capacity, tokens.shape[1])


def local(tokens, expert_ids, weight, mask_bits, damping):
    group_count = lax.axis_size(("expert", "hrow"))
    local_experts = weight.shape[0]
    feat_width = tokens.shape[1]
    slab_rows = weight.shape[1]
    packed = route_rows(tokens, expert_ids, group_count, local_experts)
    keep_flags = unpack_bits(mask_bits)
    keep_mask = keep_flags[None, :, :] == 1
    pruned = jnp.where(keep_mask, jnp.zeros_like(weight), weight)
    block = lax.all_to_all(packed, ("expert", "hrow"), split_axis=1, concat_axis=2, tiled=True)
    partials = jnp.einsum("esf,exgcf->exgcs", pruned, block, preferred_element_type=jnp.float32)
    slot_count = block.shape[1] * block.shape[2] * block.shape[3]
    routed = block.reshape(local_experts, slot_count, feat_width)
    partials = partials.reshape(local_experts, slot_count, slab_rows)
    projected = lax.psum(partials, "hcol").astype(jnp.bfloat16)
    comp_term = (
        jnp.einsum("ers,erf->esf", projected, routed, preferred_element_type=jnp.float32) / ROWS_E
    )
    diag_scale = (
        jnp.einsum("erf,erf->ef", routed, routed, preferred_element_type=jnp.float32) / ROWS_E
        + damping
    )
    updated = weight.astype(jnp.float32) + ETA * comp_term / diag_scale[:, None, :]
    return jnp.where(keep_mask, updated, jnp.float32(0.0)).astype(jnp.bfloat16)


MESH = pl.DeviceIdType.MESH
FLAGS = 128
CHUNK = 256
WIDE = 512
PIECES = 4


def kernel(tok_hbm, ids_hbm, w_hbm, bits_hbm, damp_hbm, out_hbm,
           held, w_ref, pruned, keep, part, other, squares, ids_ref, wide_ids, bits_ref, words, damp_ref, out_ref,
           load_sem, recv_sem, x_sem, core_sem, mate_sem, across_sem, y_send, y_recv, store_sem):
    z, cross, y = lax.axis_index("expert"), lax.axis_index("hrow"), lax.axis_index("hcol")
    tok_count, feat = tok_hbm.shape
    slab = w_hbm.shape[1]
    quarter = feat // (128 * PIECES) * 128
    spans = [(i * quarter, quarter) for i in range(PIECES - 1)]
    spans.append(((PIECES - 1) * quarter, feat + FLAGS - (PIECES - 1) * quarter))
    whole = (0, feat + FLAGS)
    x, core = cross // 2, cross % 2
    upper = z // 2
    inner = (z + 1) // 2 % 2
    mate = 4 * upper + 1 - z
    across = 3 - z
    order = (z, mate, 2 - upper, 3 - 3 * upper)
    x_row, core_row = (1 - x) * 2 + core, x * 2 + 1 - core
    both_row = (1 - x) * 2 + 1 - core
    to_mate, to_across = (mate, cross, y), (across, cross, y)
    to_x, to_core, to_y = (z, x_row, y), (z, core_row, y), (z, cross, 1 - y)
    mine = z * 4 + cross

    loads = [
        pltpu.make_async_copy(tok_hbm, held.at[mine, :, pl.ds(0, feat)], load_sem.at[0]),
        pltpu.make_async_copy(ids_hbm, ids_ref, load_sem.at[1]),
        pltpu.make_async_copy(bits_hbm, bits_ref.at[pl.ds(0, bits_hbm.shape[0]), :], load_sem.at[2]),
        pltpu.make_async_copy(w_hbm.at[0], w_ref, load_sem.at[3]),
        pltpu.make_async_copy(damp_hbm, damp_ref, load_sem.at[4]),
    ]
    barrier = pltpu.get_barrier_semaphore()
    for device in (to_mate, to_x, to_core, to_y):
        pl.semaphore_signal(barrier, inc=1, device_id=device, device_id_type=MESH)

    @pl.when(inner == 1)
    def _():
        pl.semaphore_signal(barrier, inc=1, device_id=to_across, device_id_type=MESH)

    for load in loads:
        load.start()

    def block(number, h, sem, device):
        lo, size = whole if h is None else spans[h]
        piece = held.at[number, :, pl.ds(lo, size)]
        return pltpu.make_async_remote_copy(
            src_ref=piece, dst_ref=piece, send_sem=sem, recv_sem=recv_sem.at[number, h or 0],
            device_id=device, device_id_type=MESH)

    def arrived(number, h):
        block(number, h, x_sem.at[0, 0], to_x).wait_recv()

    sent = {None: [], 0: [], 1: []}
    own_column = [order[step] * 4 + cross for step in range(4)]
    other_column = [order[step] * 4 + x_row for step in range(4)]

    def send(number, h, sem, at, device, where=None):
        block(number, h, sem.at[at], device).start()
        sent[where].append((number, h, sem, at, device))

    def send_on(kind, number, h, sem, at, device):
        @pl.when(inner == kind)
        def _():
            send(number, h, sem, at, device, kind)

    def finish(where):
        for number, h, sem, at, device in sent[where]:
            block(number, h, sem.at[at], device).wait_send()

    def spread(h):
        send_on(1, mine, h, across_sem, (0, h), to_across)
        send(mine, h, mate_sem, (0, h), to_mate)
        send(mine, h, x_sem, (0, h), to_x)

    def column(step, h, where=None):
        number = own_column[step]
        arrived(number, h)
        if where != 0:
            sem, device = (across_sem, to_across) if step == 1 else (mate_sem, to_mate)
            at = (1, h) if step == 1 else (step, h)
            if where == 1:
                send(number, h, sem, at, device, 1)
            else:
                send_on(1, number, h, sem, at, device)
        if step > 1 or (where == 0 and h < PIECES // 2):
            send(number, h, x_sem, (step, h), to_x, where)

    def to_other_core(step):
        send(own_column[step], None, core_sem, (step, 0), to_core)

    def crossed(step):
        for h in range(PIECES):
            arrived(other_column[step], h)
            if step == 3:
                send(other_column[step], h, core_sem, (4 + step, h), to_core)
        if step < 3:
            send(other_column[step], None, core_sem, (4 + step, 0), to_core)

    def rows_of(first, count):
        return pl.ds(pl.multiple_of(first * tok_count, tok_count), count * tok_count)

    def y_copy(first, count, which):
        rows = rows_of(first, count)
        return pltpu.make_async_remote_copy(
            src_ref=part.at[rows, :], dst_ref=other.at[rows, :], send_sem=y_send.at[which],
            recv_sem=y_recv.at[which], device_id=to_y, device_id_type=MESH)

    def member(flags):
        lane = lax.broadcasted_iota(jnp.int32, flags.shape, 1)
        return jnp.sum(jnp.where(lane == mine, flags.astype(jnp.float32), 0.0), axis=1, keepdims=True)

    summed = []

    def project(first, count):
        rows, blocks = count * tok_count, pl.ds(first, count)
        tokens = held[blocks, :, 0:feat].reshape(rows, feat)
        part[rows_of(first, count), :] = lax.dot_general(
            pruned[...], tokens, (((1,), (1,)), ((), ())), preferred_element_type=jnp.float32).T
        copy = y_copy(first, count, len(summed))
        copy.start()
        summed.append(copy)
        here = member(held[blocks, :, feat:feat + FLAGS].reshape(rows, FLAGS))
        for lo in range(0, feat, CHUNK):
            piece = held[blocks, :, lo:lo + CHUNK].reshape(rows, CHUNK).astype(jnp.float32)
            total = jnp.sum((piece * piece * here).reshape(-1, 8, CHUNK), axis=0)
            squares[:, lo:lo + CHUNK] = total if len(summed) == 1 else squares[:, lo:lo + CHUNK] + total

    def other_core(step, row):
        for h in range(PIECES) if step == 3 and row is both_row else (None,):
            arrived(order[step] * 4 + row, h)

    def plane(step):
        other_core(step, core_row)
        other_core(step, both_row)
        project(order[step] * 4, 4)

    loads[1].wait()
    wide_ids[...] = jnp.full_like(wide_ids, -1)
    wide_ids[:, 0:tok_count] = ids_ref[...]
    expert = lax.broadcasted_iota(jnp.int32, (FLAGS, 128), 0)
    named = jnp.zeros((FLAGS, 128), jnp.float32)
    for k in range(ids_ref.shape[0]):
        named = jnp.where(wide_ids[k:k + 1, :] == expert, 1.0, named)
    held[mine, :, feat:feat + FLAGS] = named.T[0:tok_count, :].astype(jnp.bfloat16)
    loads[0].wait()
    pl.semaphore_wait(barrier, 4 + inner)

    for h in range(PIECES):
        spread(h)
    to_other_core(0)

    filled = bits_hbm.shape[0]
    if filled < 128:
        bits_ref[filled:128, :] = jnp.zeros((128 - filled, slab), jnp.int32)
    loads[2].wait()
    loads[3].wait()
    words[...] = bits_ref[...].T

    spot = lax.broadcasted_iota(jnp.int32, (1, 128), 1)
    group = jnp.right_shift(spot, 5)
    probe = jnp.left_shift(jnp.int32(1), jnp.bitwise_and(spot, 31))

    def unpack(j, carry):
        at = pl.ds(pl.multiple_of(j * 128, 128), 128)
        index = jnp.broadcast_to(group + 4 * j, (slab, 128))
        word = jnp.take_along_axis(words[...], index, axis=1)
        flag = jnp.where(jnp.bitwise_and(word, probe) != 0, 1.0, 0.0).astype(jnp.bfloat16)
        keep[:, at] = flag
        pruned[:, at] = w_ref[:, at] * (jnp.bfloat16(1.0) - flag)
        return carry

    steps = feat // 128
    lax.fori_loop(0, steps, unpack, 0)
    @pl.when(inner == 1)
    def _():
        for h in range(PIECES):
            column(1, h, 1)
            column(2, h, 1)
        for h in range(PIECES):
            arrived(other_column[0], h)

    @pl.when(inner == 0)
    def _():
        for h in range(PIECES):
            column(1, h, 0)
            arrived(other_column[0], h)
            send(other_column[0], h, mate_sem, (1, h), to_mate, 0)
        for h in range(PIECES):
            column(2, h, 0)

    to_other_core(1)
    to_other_core(2)
    send(other_column[0], None, core_sem, (4, 0), to_core)
    for h in range(PIECES):
        column(3, h)
    for h in range(PIECES // 2, PIECES):
        send_on(1, other_column[0], h, mate_sem, (1, h), to_mate)
    to_other_core(3)
    crossed(2)
    plane(0)
    crossed(3)
    crossed(1)
    plane(2)
    other_core(3, core_row)
    project(order[3] * 4 + 2 * x, 2)
    plane(1)
    other_core(3, both_row)
    project(order[3] * 4 + 2 * (1 - x), 2)

    loads[4].wait()
    here = member(held[:, :, feat:feat + FLAGS].reshape(-1, FLAGS))
    for copy in summed:
        copy.wait_recv()
    projected = jnp.where(here > 0.5, part[...] + other[...], 0.0).T.astype(jnp.bfloat16)
    stores = []
    for lo in range(0, feat, WIDE):
        at = slice(lo, lo + WIDE)
        routed = held[:, :, at].reshape(-1, WIDE)
        comp = jnp.dot(projected, routed, preferred_element_type=jnp.float32)
        diag = jnp.sum(squares[:, at], axis=0, keepdims=True) / ROWS_E + damp_ref[:, at]
        updated = w_ref[:, at].astype(jnp.float32) + comp * (ETA / ROWS_E / diag)
        out_ref[:, at] = updated.astype(jnp.bfloat16) * keep[:, at]
        store = pltpu.make_async_copy(out_ref.at[:, at], out_hbm.at[0, :, at], store_sem.at[lo // WIDE])
        store.start()
        stores.append(store)

    finish(None)
    for copy in summed:
        copy.wait_send()

    @pl.when(inner == 1)
    def _():
        finish(1)

    @pl.when(inner == 0)
    def _():
        finish(0)

    for store in stores:
        store.wait()


def leave(from_hbm, to_hbm, slabs, in_sems, out_sems):
    count, rows = slabs.shape[0], slabs.shape[1]
    ins, outs = [], []
    for i in range(count):
        at = pl.ds(i * rows, rows)
        ins.append(pltpu.make_async_copy(from_hbm.at[0, at, :], slabs.at[i], in_sems.at[i]))
        outs.append(pltpu.make_async_copy(slabs.at[i], to_hbm.at[0, at, :], out_sems.at[i]))
        ins[i].start()
    for i in range(count):
        ins[i].wait()
        outs[i].start()
    for out in outs:
        out.wait()


def gathered(tokens, expert_ids, weight, mask_bits, damping):
    tok_count, feat = tokens.shape
    slab = weight.shape[1]
    blocks = 16
    total = blocks * tok_count
    dma = pltpu.SemaphoreType.DMA
    result = pl.pallas_call(
        kernel,
        out_shape=jax.ShapeDtypeStruct(weight.shape, jnp.bfloat16),
        in_specs=[pl.BlockSpec(memory_space=pltpu.HBM)] * 5,
        out_specs=pl.BlockSpec(memory_space=pl.ANY),
        scratch_shapes=[
            pltpu.VMEM((blocks, tok_count, feat + FLAGS), jnp.bfloat16),
            pltpu.VMEM((slab, feat), jnp.bfloat16),
            pltpu.VMEM((slab, feat), jnp.bfloat16),
            pltpu.VMEM((slab, feat), jnp.bfloat16),
            pltpu.VMEM((total, slab), jnp.float32),
            pltpu.VMEM((total, slab), jnp.float32),
            pltpu.VMEM((8, feat), jnp.float32),
            pltpu.VMEM((expert_ids.shape[1], tok_count), jnp.int32),
            pltpu.VMEM((expert_ids.shape[1], 128), jnp.int32),
            pltpu.VMEM((128, slab), jnp.int32),
            pltpu.VMEM((slab, 128), jnp.int32),
            pltpu.VMEM((1, feat), jnp.float32),
            pltpu.VMEM((slab, feat), jnp.bfloat16),
            dma((5,)),
            dma((blocks, PIECES)),
            dma((4, PIECES)),
            dma((8, PIECES)),
            dma((4, PIECES)),
            dma((2, PIECES)),
            dma((5,)),
            dma((5,)),
            dma((feat // WIDE,)),
        ],
        compiler_params=pltpu.CompilerParams(
            collective_id=0, has_side_effects=True, vmem_limit_bytes=62 * 1024 * 1024),
        cost_estimate=pl.CostEstimate(
            flops=4 * total * slab * feat, bytes_accessed=4 * slab * feat, transcendentals=0),
    )(tokens, expert_ids.T, weight, mask_bits.T, damping)
    return pl.pallas_call(
        leave,
        out_shape=jax.ShapeDtypeStruct(weight.shape, jnp.bfloat16),
        in_specs=[pl.BlockSpec(memory_space=pl.ANY)],
        out_specs=pl.BlockSpec(memory_space=pl.ANY),
        scratch_shapes=[pltpu.VMEM((8, slab // 8, feat), jnp.bfloat16), dma((8,)), dma((8,))],
        compiler_params=pltpu.CompilerParams(vmem_limit_bytes=62 * 1024 * 1024),
    )(result)


def solution(mesh):
    in_specs = (
        P(("expert", "hrow"), "hcol"),
        P(("expert", "hrow"), None),
        P(("expert", "hrow"), None, "hcol"),
        P(None, "hcol"),
        P(("expert", "hrow"), "hcol"),
    )
    out_specs = P(("expert", "hrow"), None, "hcol")
    line, cross = mesh.shape["expert"], mesh.shape["hrow"]

    def body(tokens, expert_ids, weight, mask_bits, damping):
        tok_count, top_count = expert_ids.shape
        capacity = 2 * tok_count * top_count // (line * cross * weight.shape[0])
        fits = line == 4 and cross == 4 and mesh.shape["hcol"] == 2 and weight.shape[0] == 1
        if fits and capacity >= tok_count:
            return gathered(tokens, expert_ids, weight, mask_bits, damping)
        return local(tokens, expert_ids, weight, mask_bits, damping)

    return jax.shard_map(body, mesh=mesh, in_specs=in_specs, out_specs=out_specs, check_vma=False)
```
